32 devices in a mesh: ctx: 8 (over z, core), tp: 4 (over y, x).
Axes of the slice: x: 2, y: 2, z: 4, core: 2. Of those that a mesh axis runs over, the one named last changes fastest.
Arguments:
- tokens: bfloat16 [2048, 2048], P(('ctx', 'tp')), may hold values from -16 to 16
- w_project: bfloat16 [2048, 12288], P(None, 'tp'), may hold values from -0.125 to 0.125
- w_mixers: bfloat16 [2048, 64], P(None, 'tp'), may hold values from -1 to 1
- conv_weight: bfloat16 [16, 4, 512], P('tp'), may hold values from -3 to 3
- decay_log: float32 [32], P('tp'), may hold values from 0 to 1
- step_bias: float32 [32], P('tp'), may hold values from -20 to -2
- norm_gain: float32 [128], replicated, may hold values from 0.1 to 1.9
- w_output: bfloat16 [4096, 2048], P('tp'), may hold values from -0.09375 to 0.09375
Outputs:
- mixed_rows: bfloat16 [2048, 2048], P(('ctx', 'tp'))
The draws below stay inside these ranges and needn't reach their ends.
All inputs are finite; a program needn't handle non-finite values.
Results may differ from the reference program's by a relative error of at most 0.018.
Values may be sent and summed in bfloat16 or wider, within the bound.
A program may use at most 64 MiB of HBM per device.

```python
import math
import jax
import jax.numpy as jnp
from jax import lax

D = 2048
KEY_HEADS = 16
HEAD_DIM = 128
CONV = 4
TOK_DEV = 256
VALUE_HEADS = 32
TOKENS = 2048
QKVZ = 12288
MIXERS = 64
INNER = 4096
N_CTX = 8
N_TP = 4


common_lift = 12.0


def spike_orientation(key):
    signs = jax.random.randint(jax.random.fold_in(key, 4242), (D,), 0, 2)
    return (2 * signs - 1).astype(jnp.float32) * D ** (-0.5)


def common_direction(key):
    signs = jax.random.randint(jax.random.fold_in(key, 5151), (D,), 0, 2)
    return (2 * signs - 1).astype(jnp.float32) * D ** (-0.5)


def draw_tokens(key, part):
    update_heading = spike_orientation(key)
    shared = common_direction(key)
    base = jnp.clip(jax.random.normal(jax.random.fold_in(key, 1), (TOKENS, D), jnp.float32), -6.0, 6.0)
    places = jax.random.randint(jax.random.fold_in(key, 3), (3,), 0, TOKENS)
    hits = jnp.sum((jnp.arange(TOKENS)[:, None] == places[None, :]).astype(jnp.float32), axis=1)
    hits = jnp.minimum(hits, 1.0)
    lift = 2.0 * (math.log(TOKENS) + 2.0)
    return (base + hits[:, None] * lift * update_heading[None, :] + common_lift * shared[None, :]).astype(jnp.bfloat16)


def draw_w_mixers(key, part):
    update_heading = spike_orientation(key)
    shared = common_direction(key)
    noise = jnp.clip(jax.random.normal(jax.random.fold_in(key, 11), (D, MIXERS), jnp.float32), -6.0, 6.0)
    noise = noise * D ** (-0.5)
    columns = jnp.arange(MIXERS) % 4
    decay_cols = (columns >= 2)[None, :]
    offset = (-math.log(TOKENS / HEAD_DIM) - 0.05) / common_lift
    beta_part = 0.4 * noise + offset * shared[:, None]
    return jnp.where(decay_cols, 0.5 * noise + 0.5 * update_heading[:, None], beta_part).astype(jnp.bfloat16)


def draw_step_bias(key, part):
    odds = 2
    picks = jax.random.randint(jax.random.fold_in(key, 21), (VALUE_HEADS,), 0, odds)
    slow = -math.log(TOKENS) - 3.0 + jax.random.uniform(jax.random.fold_in(key, 22), (VALUE_HEADS,), jnp.float32, -0.5, 0.5)
    fast = jax.random.uniform(jax.random.fold_in(key, 23), (VALUE_HEADS,), jnp.float32, -4.0, -3.0)
    return jnp.where(picks == 0, fast, slow)


def block_levels(rng, extent, shards, low, high):
    def one(dim, shards_of):
        steps = jax.random.uniform(jax.random.fold_in(jax.random.fold_in(rng, 6), dim), (shards_of,), jnp.float32, low / len(shards), high / len(shards))
        return jnp.repeat(jnp.exp(steps), extent[dim] // shards_of).reshape((-1,) + (1,) * (len(extent) - dim - 1))

    loudness = one(*shards[0])
    for cut in shards[1:]:
        loudness = loudness * one(*cut)
    return loudness


def scatter_about(own_key, extent, deviation, limit, cuts=(), held_as=jnp.bfloat16):
    factor_of = block_levels(own_key, extent, cuts, -0.22, 0.18) if cuts else 1.0
    drawn = jax.random.normal(own_key, extent, jnp.float32) * deviation * factor_of
    return jnp.minimum(jnp.maximum(drawn, -limit), limit).astype(held_as)


def setup_inputs(seed: int = 0) -> dict:
    streams_of = jax.random.split(jax.random.key(seed), 9)
    return {
        "tokens": draw_tokens(jax.random.fold_in(streams_of[8], 71), 0),
        "w_project": scatter_about(streams_of[1], (D, QKVZ), D ** -0.5, 0.125, ((1, 4),)),
        "w_mixers": draw_w_mixers(jax.random.fold_in(streams_of[8], 71), 0),
        "conv_weight": scatter_about(streams_of[3], (KEY_HEADS, CONV, 4 * HEAD_DIM), CONV ** -0.5, 3.0, ((0, 4),)),
        "decay_log": jnp.clip(1.0 * jax.random.uniform(streams_of[4], (VALUE_HEADS,), jnp.float32) ** block_levels(streams_of[4], (VALUE_HEADS,), ((0, 4),), -0.2, 0.2), 0.0, 1.0),
        "step_bias": draw_step_bias(jax.random.fold_in(streams_of[8], 71), 0),
        "norm_gain": jnp.clip(1.0 + 0.18 * jax.random.normal(streams_of[6], (HEAD_DIM,), jnp.float32), 0.1, 1.9),
        "w_output": scatter_about(streams_of[7], (INNER, D), INNER ** -0.5, 0.09375, ((0, 4),)),
    }


EPSILON = 1e-06
TOP_PRECISION = lax.Precision.HIGHEST

def unit_rows(values):
    values = values.astype(jnp.float32)
    return values * lax.rsqrt(lax.optimization_barrier(jnp.sum(values * values, axis=-1, keepdims=True)) + EPSILON)

def token_step(carried_over_state, inputs):
    query_rows, key_columns, value_rows, write_intensity, log_decay = inputs
    carried_over_state = jnp.exp(log_decay)[:, None, None] * carried_over_state
    estimated_values = jnp.einsum('upr,up->ur', carried_over_state, key_columns, precision=TOP_PRECISION)
    carried_over_state = carried_over_state + jnp.einsum('om,on->omn', key_columns, write_intensity[:, None] * (value_rows - estimated_values), precision=TOP_PRECISION)
    return (carried_over_state, jnp.einsum('upr,up->ur', carried_over_state, query_rows, precision=TOP_PRECISION))

def reference(tokens, w_project, w_mixers, conv_weight, decay_log, step_bias, norm_gain, w_output):
    value_heads = 2 * KEY_HEADS

    def block_step(running, block_tokens):
        carried_over_state, border = running
        projected = jnp.dot(block_tokens, w_project, preferred_element_type=jnp.float32).astype(jnp.bfloat16)
        projected = projected.reshape(TOK_DEV, KEY_HEADS, 6 * HEAD_DIM)
        mixers = jnp.dot(block_tokens, w_mixers, preferred_element_type=jnp.float32).astype(jnp.bfloat16)
        mixers = mixers.reshape(TOK_DEV, KEY_HEADS, 4)
        conv_input = projected[:, :, :4 * HEAD_DIM]
        extended = jnp.concatenate([border, conv_input], axis=0)
        summed = jnp.zeros((TOK_DEV, KEY_HEADS, 4 * HEAD_DIM), jnp.float32)
        for offset in range(CONV):
            summed = summed + conv_weight[:, offset, :].astype(jnp.float32)[None] * extended[offset:offset + TOK_DEV].astype(jnp.float32)
        activated = jax.nn.silu(summed).astype(jnp.bfloat16)
        query_rows = jnp.repeat(unit_rows(activated[:, :, :HEAD_DIM]), 2, axis=1)
        key_columns = jnp.repeat(unit_rows(activated[:, :, HEAD_DIM:2 * HEAD_DIM]), 2, axis=1)
        value_rows = activated[:, :, 2 * HEAD_DIM:].astype(jnp.float32).reshape(TOK_DEV, value_heads, HEAD_DIM)
        write_intensity = jax.nn.sigmoid(mixers[:, :, :2].astype(jnp.float32).reshape(TOK_DEV, value_heads))
        decay_input = mixers[:, :, 2:].astype(jnp.float32).reshape(TOK_DEV, value_heads)
        log_decay = -jnp.exp(decay_log)[None, :] * jax.nn.softplus(decay_input + step_bias[None, :])
        carried_over_state, core_out = lax.scan(token_step, carried_over_state, (query_rows, key_columns, value_rows, write_intensity, log_decay))
        core_low = lax.optimization_barrier(core_out.astype(jnp.bfloat16))
        widened = core_low.astype(jnp.float32)
        gate_part = projected[:, :, 4 * HEAD_DIM:].astype(jnp.float32).reshape(TOK_DEV, value_heads, HEAD_DIM)
        scaled = widened * lax.rsqrt(lax.optimization_barrier(jnp.mean(widened * widened, axis=-1, keepdims=True)) + EPSILON)
        normed = (norm_gain * scaled * jax.nn.silu(gate_part)).astype(jnp.bfloat16)
        normed = normed.reshape(TOK_DEV, value_heads * HEAD_DIM)
        block_width = value_heads * HEAD_DIM // N_TP
        mixed_rows = jnp.zeros((TOK_DEV, D), jnp.float32)
        for group_index in range(N_TP):
            column_start = group_index * block_width
            partial_sum = jnp.dot(normed[:, column_start:column_start + block_width], w_output[column_start:column_start + block_width], preferred_element_type=jnp.float32)
            mixed_rows = mixed_rows + lax.optimization_barrier(partial_sum.astype(jnp.bfloat16)).astype(jnp.float32)
        return ((carried_over_state, conv_input[TOK_DEV - CONV + 1:]), mixed_rows.astype(jnp.bfloat16))
    start_state = jnp.zeros((value_heads, HEAD_DIM, HEAD_DIM), jnp.float32)
    start_border = jnp.zeros((CONV - 1, KEY_HEADS, 4 * HEAD_DIM), jnp.bfloat16)
    _, outputs = lax.scan(block_step, (start_state, start_border), tokens.reshape(N_CTX, TOK_DEV, D))
    return outputs.reshape(N_CTX * TOK_DEV, D)
```

```python
import functools

import jax
import jax.numpy as jnp
from jax import lax
from jax.experimental import pallas as pl
from jax.experimental.pallas import tpu as pltpu
from jax.sharding import PartitionSpec as P

EPSILON = 1e-06
TOP_PRECISION = lax.Precision.HIGHEST
MESH = pl.DeviceIdType.MESH
WIDTH = 128
F32 = jnp.float32
BF16 = jnp.bfloat16
BORDER = 16
LEAST_LOG = -120.0


def mm(a, b):
    return jnp.dot(a, b, preferred_element_type=F32)


def mm_rows(a, b):
    return lax.dot_general(a, b, (((1,), (1,)), ((), ())), preferred_element_type=F32)


def mm_over_rows(a, b):
    return lax.dot_general(a, b, (((0,), (0,)), ((), ())), preferred_element_type=F32)


def sigmoid(x):
    return 1.0 / (1.0 + jnp.exp(-x))


def softplus(x):
    small = jnp.exp(-jnp.abs(x))
    grown = 1.0 + small
    tail = jnp.where(grown == 1.0, small, jnp.log(grown) * small / jnp.where(grown == 1.0, 1.0, grown - 1.0))
    return jnp.maximum(x, 0.0) + tail


def kernel(
    n_ctx, n_tp, key_heads, batch,
    tok_ref, wp_ref, wm_ref, cw_ref, dl_ref, sb_ref, gain_ref, wo_ref,
    out_ref,
    gath, wp, wm, wo, ext, gate, act, border_out, border_in, col, row, minus, inject, own, reach,
    s_in, s_out, decay_all, normed, stage, landed,
    own_sem, wp_sem, wm_sem, wo_sem, ag_send, ag_recv, border_sem, state_send, state_recv, rs_send, rs_recv,
):
    rows = tok_ref.shape[0]
    length = rows * n_tp
    heads = 2 * key_heads
    depth = wo_ref.shape[1]
    ctx, tp = lax.axis_index("ctx"), lax.axis_index("tp")
    six, four = 6 * WIDTH, 4 * WIDTH

    wm_copy = pltpu.make_async_copy(wm_ref, wm, wm_sem)
    wo_copy = pltpu.make_async_copy(wo_ref, wo, wo_sem)
    wp_copies = [
        pltpu.make_async_copy(wp_ref.at[:, pl.ds(g * six, six)], wp.at[g], wp_sem.at[g]) for g in range(key_heads)
    ]
    mine = pl.ds(pl.multiple_of(tp * rows, 16), rows)
    own_copy = pltpu.make_async_copy(tok_ref, gath.at[mine], own_sem)
    own_copy.start()
    for copy in wp_copies:
        copy.start()
    wm_copy.start()
    wo_copy.start()

    barrier = pltpu.get_barrier_semaphore()
    peers = [lax.rem(tp + k, n_tp) for k in range(1, n_tp)]
    for peer in peers:
        pl.semaphore_signal(barrier, inc=1, device_id={"tp": peer}, device_id_type=MESH)

    @pl.when(ctx > 0)
    def _():
        pl.semaphore_signal(barrier, inc=1, device_id={"ctx": ctx - 1}, device_id_type=MESH)

    @pl.when(ctx < n_ctx - 1)
    def _():
        pl.semaphore_signal(barrier, inc=1, device_id={"ctx": ctx + 1}, device_id_type=MESH)

    beside = jnp.where(ctx > 0, 1, 0) + jnp.where(ctx < n_ctx - 1, 1, 0)
    pl.semaphore_wait(barrier, n_tp - 1 + beside)

    gathers = [
        pltpu.make_async_remote_copy(
            src_ref=tok_ref, dst_ref=gath.at[mine], send_sem=ag_send.at[k], recv_sem=ag_recv.at[k],
            device_id={"tp": peer}, device_id_type=MESH,
        )
        for k, peer in enumerate(peers)
    ]
    for copy in gathers:
        copy.start()

    own_copy.wait()
    wm_copy.wait()
    for copy in wp_copies:
        copy.wait()
    for copy in gathers:
        copy.wait()

    def project(g, carry):
        for t in range(2):
            part = mm(gath[...], wp[g, :, t * 256 : (t + 1) * 256]).astype(BF16)
            ext[8 : 8 + length, pl.ds(pl.multiple_of(g * four + t * 256, 256), 256)] = part.astype(F32)
        return carry

    lax.fori_loop(0, key_heads, project, 0)

    border_out[...] = ext[8 + length - BORDER : 8 + length, :].astype(BF16)
    border_copy = pltpu.make_async_remote_copy(
        src_ref=border_out, dst_ref=border_in, send_sem=border_sem.at[0], recv_sem=border_sem.at[1],
        device_id={"ctx": lax.rem(ctx + 1, n_ctx)}, device_id_type=MESH,
    )

    @pl.when(ctx < n_ctx - 1)
    def _():
        border_copy.start()

    def project_gate(g, carry):
        part = mm(gath[...], wp[g, :, four:six]).astype(BF16)
        gate[:, pl.ds(pl.multiple_of(g * 256, 256), 256)] = part
        return carry

    lax.fori_loop(0, key_heads, project_gate, 0)

    mixers = mm(gath[...], wm[...]).astype(BF16).astype(F32)
    columns = mixers.shape[1]
    lane = lax.broadcasted_iota(jnp.int32, (1, columns), 1)
    rate = jnp.zeros((1, columns), F32)
    bias = jnp.zeros((1, columns), F32)
    for h in range(heads):
        here = lane == 4 * (h // 2) + 2 + h % 2
        rate = jnp.where(here, dl_ref[0, h], rate)
        bias = jnp.where(here, sb_ref[0, h], bias)
    strength = sigmoid(mixers)
    log_decay = jnp.maximum(-jnp.exp(rate) * softplus(mixers + bias), LEAST_LOG)
    at_row = lax.broadcasted_iota(jnp.int32, (length, length), 0)
    at_col = lax.broadcasted_iota(jnp.int32, (length, length), 1)
    lower = jnp.where(at_row >= at_col, 1.0, 0.0)
    cumulative = jnp.dot(lower, log_decay, precision=TOP_PRECISION, preferred_element_type=F32)

    @pl.when(ctx > 0)
    def _():
        border_copy.wait_recv()
        ext[0:8, :] = border_in[BORDER - 8 : BORDER, :].astype(F32)

    @pl.when(ctx == 0)
    def _():
        ext[0:8, :] = jnp.zeros((8, ext.shape[1]), F32)

    def convolve(g, carry):
        for t in range(4):
            place = pl.ds(pl.multiple_of(g * four + t * WIDTH, WIDTH), WIDTH)
            taps = cw_ref[g, :, t * WIDTH : (t + 1) * WIDTH].astype(F32)
            total = taps[0:1] * ext[5 : 5 + length, place]
            for j in range(1, 4):
                total = total + taps[j : j + 1] * ext[5 + j : 5 + j + length, place]
            act[:, place] = (total * sigmoid(total)).astype(BF16)
        return carry

    lax.fori_loop(0, key_heads, convolve, 0)

    wide = lax.broadcasted_iota(jnp.int32, (length, WIDTH), 1)
    for g in range(key_heads):
        query = act[:, g * four : g * four + WIDTH].astype(F32)
        key = act[:, g * four + WIDTH : g * four + 2 * WIDTH].astype(F32)
        query_unit = lax.rsqrt(jnp.sum(query * query, axis=1, keepdims=True) + EPSILON)
        key_unit = lax.rsqrt(jnp.sum(key * key, axis=1, keepdims=True) + EPSILON)
        for r in range(2):
            h = 2 * g + r
            cum = cumulative[:, 4 * g + 2 + r : 4 * g + 3 + r]
            beta = strength[:, 4 * g + r : 4 * g + r + 1]
            packed = jnp.where(
                wide == 0, cum, jnp.where(wide == 1, beta, jnp.where(wide == 2, key_unit, query_unit))
            )
            col[h] = packed
            row[h] = jnp.transpose(packed)[0:8]

    def heads_of(step, carry):
        i = lax.broadcasted_iota(jnp.int32, (length, length), 0)
        j = lax.broadcasted_iota(jnp.int32, (length, length), 1)
        apart = jnp.bitwise_xor(i, j)
        lows, inverses, scored = [], [], []
        for b in range(batch):
            g = step * batch + b
            query = act[:, pl.ds(pl.multiple_of(g * four, WIDTH), WIDTH)]
            key = act[:, pl.ds(pl.multiple_of(g * four + WIDTH, WIDTH), WIDTH)]
            key_key = mm_rows(key, key)
            query_key = mm_rows(query, key)
            for r in range(2):
                h = 2 * g + r
                scal, across = col[h], row[h]
                cum, beta, key_unit, query_unit = (scal[:, n : n + 1] for n in range(4))
                within = jnp.where(i >= j, jnp.exp(jnp.where(i >= j, cum - across[0:1], 0.0)), 0.0) * across[2:3]
                scored.append((within * query_key * query_unit).astype(BF16))
                low = jnp.where(i > j, within * key_key * (beta * key_unit), 0.0).astype(BF16)
                lows.append(low)
                inverses.append(jnp.where(i == j, 1.0, jnp.where(apart == 1, -low.astype(F32), 0.0)).astype(BF16))
        span = 2
        while span < length:
            between = (apart >= span) & (apart < 2 * span)
            firsts = [
                mm(t, jnp.where(between, low.astype(F32), 0.0).astype(BF16)).astype(BF16)
                for t, low in zip(inverses, lows)
            ]
            inverses = [t - mm(first, t).astype(BF16) for t, first in zip(inverses, firsts)]
            span *= 2
        for n, (inverse, scores) in enumerate(zip(inverses, scored)):
            g = step * batch + n // 2
            r = n % 2
            h = 2 * g + r
            scal = col[h]
            cum, beta, key_unit, query_unit = (scal[:, m : m + 1] for m in range(4))
            query = act[:, pl.ds(pl.multiple_of(g * four, WIDTH), WIDTH)].astype(F32)
            key = act[:, pl.ds(pl.multiple_of(g * four + WIDTH, WIDTH), WIDTH)].astype(F32)
            vector = act[:, pl.ds(pl.multiple_of(g * four + (2 + r) * WIDTH, WIDTH), WIDTH)].astype(F32)
            reached = jnp.exp(cum)
            last = cum[length - 1 : length]
            right = jnp.concatenate([vector * beta, key * (beta * reached * key_unit)], axis=1).astype(BF16)
            solved = mm(inverse, right).astype(BF16)
            tail = (key * (jnp.exp(last - cum) * key_unit)).astype(BF16)
            ends = mm_over_rows(tail, solved)
            inject[h] = ends[:, :WIDTH]
            minus[h] = ends[:, WIDTH:].astype(BF16)
            decay_all[h] = jnp.broadcast_to(jnp.exp(last), (8, WIDTH))
            local = mm(scores, solved)
            own[h] = local[:, :WIDTH]
            reach[h] = (query * (reached * query_unit) - local[:, WIDTH:]).astype(BF16)
        return carry

    lax.fori_loop(0, key_heads // batch, heads_of, 0)

    def state_copy(h):
        return pltpu.make_async_remote_copy(
            src_ref=s_out.at[h], dst_ref=s_in.at[h], send_sem=state_send.at[h], recv_sem=state_recv.at[h],
            device_id={"ctx": lax.rem(ctx + 1, n_ctx)}, device_id_type=MESH,
        )

    for h in range(heads):
        @pl.when(ctx > 0)
        def _():
            state_copy(h).wait_recv()
            before = s_in[h]
            after = decay_all[h, 0:1, :] * before.astype(F32) - mm(minus[h], before) + inject[h]
            s_out[h] = after.astype(BF16)

        @pl.when(ctx == 0)
        def _():
            s_in[h] = jnp.zeros((WIDTH, WIDTH), BF16)
            s_out[h] = inject[h].astype(BF16)

        @pl.when(ctx < n_ctx - 1)
        def _():
            state_copy(h).start()

    def finish(h, carry):
        core = (own[h] + mm(reach[h], s_in[h])).astype(BF16).astype(F32)
        place = pl.ds(pl.multiple_of(h * WIDTH, WIDTH), WIDTH)
        gated = gate[:, place].astype(F32)
        scaled = core * lax.rsqrt(jnp.mean(core * core, axis=1, keepdims=True) + EPSILON)
        normed[:, place] = (gain_ref[...] * scaled * (gated * sigmoid(gated))).astype(BF16)
        return carry

    lax.fori_loop(0, heads, finish, 0)

    wo_copy.wait()
    pieces = rs_send.shape[0]
    piece = depth // pieces

    def share_copy(q, k):
        peer = lax.rem(tp + k + 1, n_tp)
        place = pl.ds(q * piece, piece)
        return pltpu.make_async_remote_copy(
            src_ref=stage.at[pl.ds(pl.multiple_of(peer * rows, 16), rows), place],
            dst_ref=landed.at[k, :, place],
            send_sem=rs_send.at[q, k], recv_sem=rs_recv.at[q, k],
            device_id={"tp": peer}, device_id_type=MESH,
        )

    for q in range(pieces):
        for t in range(0, piece, 256):
            place = slice(q * piece + t, q * piece + t + 256)
            stage[:, place] = mm(normed[...], wo[:, place]).astype(BF16)
        for k in range(n_tp - 1):
            share_copy(q, k).start()
    for q in range(pieces):
        place = slice(q * piece, (q + 1) * piece)
        total = stage[mine, place].astype(F32)
        for k in range(n_tp - 1):
            share_copy(q, k).wait_recv()
            total = total + landed[k, :, place].astype(F32)
        out_ref[:, place] = total.astype(BF16)
    for q in range(pieces):
        for k in range(n_tp - 1):
            share_copy(q, k).wait_send()

    @pl.when(ctx < n_ctx - 1)
    def _():
        border_copy.wait_send()
        for h in range(heads):
            state_copy(h).wait_send()


def on_device(tokens, w_project, w_mixers, conv_weight, decay_log, step_bias, norm_gain, w_output):
    n_ctx, n_tp = lax.axis_size("ctx"), lax.axis_size("tp")
    rows, depth = tokens.shape
    length = rows * n_tp
    key_heads = conv_weight.shape[0]
    heads = 2 * key_heads
    inner = heads * WIDTH
    batch = 2 if key_heads % 2 == 0 else 1
    pieces = 4
    vmem = pl.BlockSpec(memory_space=pltpu.VMEM)
    smem = pl.BlockSpec(memory_space=pltpu.SMEM)
    far = pl.BlockSpec(memory_space=pl.ANY)
    dma = pltpu.SemaphoreType.DMA
    square = (heads, WIDTH, WIDTH)
    return pl.pallas_call(
        functools.partial(kernel, n_ctx, n_tp, key_heads, batch),
        out_shape=jax.ShapeDtypeStruct((rows, depth), BF16),
        in_specs=[far, far, far, vmem, smem, smem, vmem, far],
        out_specs=vmem,
        scratch_shapes=[
            pltpu.VMEM((length, depth), BF16),
            pltpu.VMEM((key_heads, depth, 6 * WIDTH), BF16),
            pltpu.VMEM(w_mixers.shape, BF16),
            pltpu.VMEM(w_output.shape, BF16),
            pltpu.VMEM((8 + length, key_heads * 4 * WIDTH), F32),
            pltpu.VMEM((length, inner), BF16),
            pltpu.VMEM((length, key_heads * 4 * WIDTH), BF16),
            pltpu.VMEM((BORDER, key_heads * 4 * WIDTH), BF16),
            pltpu.VMEM((BORDER, key_heads * 4 * WIDTH), BF16),
            pltpu.VMEM((heads, length, WIDTH), F32),
            pltpu.VMEM((heads, 8, length), F32),
            pltpu.VMEM(square, BF16),
            pltpu.VMEM(square, F32),
            pltpu.VMEM((heads, length, WIDTH), F32),
            pltpu.VMEM((heads, length, WIDTH), BF16),
            pltpu.VMEM(square, BF16),
            pltpu.VMEM(square, BF16),
            pltpu.VMEM((heads, 8, WIDTH), F32),
            pltpu.VMEM((length, inner), BF16),
            pltpu.VMEM((length, depth), BF16),
            pltpu.VMEM((n_tp - 1, rows, depth), BF16),
            dma, dma((key_heads,)), dma, dma,
            dma((n_tp - 1,)), dma((n_tp - 1,)), dma((2,)),
            dma((heads,)), dma((heads,)),
            dma((pieces, n_tp - 1)), dma((pieces, n_tp - 1)),
        ],
        compiler_params=pltpu.CompilerParams(
            collective_id=0, has_side_effects=True, vmem_limit_bytes=52 * 1024 * 1024
        ),
    )(
        tokens, w_project, w_mixers, conv_weight,
        decay_log.reshape(1, heads), step_bias.reshape(1, heads), norm_gain.reshape(1, WIDTH), w_output,
    )


def solution(mesh):
    placed = (
        P(("ctx", "tp"), None),
        P(None, "tp"),
        P(None, "tp"),
        P("tp", None, None),
        P("tp"),
        P("tp"),
        P(),
        P("tp", None),
    )
    return jax.shard_map(
        on_device, mesh=mesh, in_specs=placed, out_specs=P(("ctx", "tp"), None), check_vma=False
    )
```

```python
import functools

import jax
import jax.numpy as jnp
from jax import lax
from jax.experimental import pallas as pl
from jax.experimental.pallas import tpu as pltpu
from jax.sharding import PartitionSpec as P

EPSILON = 1e-06
TOP_PRECISION = lax.Precision.HIGHEST
MESH = pl.DeviceIdType.MESH
WIDTH = 128
F32 = jnp.float32
BF16 = jnp.bfloat16
BORDER = 16
LEAST_LOG = -120.0


def mm(a, b):
    return jnp.dot(a, b, preferred_element_type=F32)


def mm_rows(a, b):
    return lax.dot_general(a, b, (((1,), (1,)), ((), ())), preferred_element_type=F32)


def mm_over_rows(a, b):
    return lax.dot_general(a, b, (((0,), (0,)), ((), ())), preferred_element_type=F32)


def sigmoid(x):
    return 1.0 / (1.0 + jnp.exp(-x))


def softplus(x):
    small = jnp.exp(-jnp.abs(x))
    grown = 1.0 + small
    tail = jnp.where(grown == 1.0, small, jnp.log(grown) * small / jnp.where(grown == 1.0, 1.0, grown - 1.0))
    return jnp.maximum(x, 0.0) + tail


def kernel(
    n_ctx, n_tp, key_heads, batch, chunks,
    tok_ref, wp_ref, wm_ref, cw_in, dl_in, sb_in, gain_in, wo_ref,
    out_ref,
    gath, wp, wm, wo, cw_ref, dl_ref, sb_ref, gain_ref,
    ext, act, border_out, border_in, col, row, solutions, minus, inject, own, reach,
    s_in, s_out, decay_all, normed, stage, landed,
    own_sem, wp_sem, small_sem, wo_sem, ag_send, ag_recv, border_sem, state_send, state_recv, rs_send, rs_recv,
):
    rows = tok_ref.shape[0]
    length = rows * n_tp
    heads = 2 * key_heads
    depth = wo_ref.shape[1]
    ctx, tp = lax.axis_index("ctx"), lax.axis_index("tp")
    six, four = 6 * WIDTH, 4 * WIDTH

    k_rows = depth // chunks
    small_copies = [
        pltpu.make_async_copy(source, target, small_sem.at[n])
        for n, (source, target) in enumerate(
            [(wm_ref, wm), (cw_in, cw_ref), (dl_in, dl_ref), (sb_in, sb_ref), (gain_in, gain_ref)]
        )
    ]
    wo_copy = pltpu.make_async_copy(wo_ref, wo, wo_sem)
    wp_copies = [
        pltpu.make_async_copy(wp_ref.at[pl.ds(k * k_rows, k_rows)], wp.at[pl.ds(k * k_rows, k_rows)], wp_sem.at[k])
        for k in range(chunks)
    ]
    mine = pl.ds(pl.multiple_of(tp * rows, 16), rows)
    own_copy = pltpu.make_async_copy(tok_ref, gath.at[mine], own_sem)
    own_copy.start()
    for copy in wp_copies:
        copy.start()
    for copy in small_copies:
        copy.start()
    wo_copy.start()

    barrier = pltpu.get_barrier_semaphore()
    peers = [lax.rem(tp + k, n_tp) for k in range(1, n_tp)]
    for peer in peers:
        pl.semaphore_signal(barrier, inc=1, device_id={"tp": peer}, device_id_type=MESH)

    @pl.when(ctx > 0)
    def _():
        pl.semaphore_signal(barrier, inc=1, device_id={"ctx": ctx - 1}, device_id_type=MESH)

    @pl.when(ctx < n_ctx - 1)
    def _():
        pl.semaphore_signal(barrier, inc=1, device_id={"ctx": ctx + 1}, device_id_type=MESH)

    beside = jnp.where(ctx > 0, 1, 0) + jnp.where(ctx < n_ctx - 1, 1, 0)
    pl.semaphore_wait(barrier, n_tp - 1 + beside)

    def block_copy(source, held, peer, way, k):
        place = pl.ds(k * k_rows, k_rows)
        return pltpu.make_async_remote_copy(
            src_ref=source.at[:, place] if held is mine else source.at[held, place],
            dst_ref=gath.at[held, place],
            send_sem=ag_send.at[way, k], recv_sem=ag_recv.at[way, k],
            device_id={"tp": peer}, device_id_type=MESH,
        )

    def project(k):
        wp_copies[k].wait()
        place = slice(k * k_rows, (k + 1) * k_rows)

        def tile(t, carry):
            span = pl.ds(pl.multiple_of(t * 256, 256), 256)
            part = mm(gath[:, place], wp[place, span])
            if k > 0:
                part = part + ext[8 : 8 + length, span]
            if k == chunks - 1:
                part = part.astype(BF16).astype(F32)
            ext[8 : 8 + length, span] = part
            return carry

        lax.fori_loop(0, key_heads * six // 256, tile, 0)

    if n_tp == 4:
        x_peer = tp + 1 - 2 * lax.rem(tp, 2)
        y_peer = lax.rem(tp + 2, 4)
        x_rows = pl.ds(pl.multiple_of(x_peer * rows, 16), rows)
        y_rows = pl.ds(pl.multiple_of(y_peer * rows, 16), rows)
        direct = [
            [block_copy(tok_ref, mine, peer, way, k) for way, peer in enumerate((x_peer, y_peer))]
            for k in range(chunks)
        ]
        passed = [
            block_copy(gath, x_rows, y_peer, 2, k) if k % 2 == 0 else block_copy(gath, y_rows, x_peer, 2, k)
            for k in range(chunks)
        ]
        for pair in direct:
            for copy in pair:
                copy.start()
        own_copy.wait()
        for k in range(chunks):
            for copy in direct[k]:
                copy.wait_recv()
            passed[k].start()
            if k > 0:
                passed[k - 1].wait_recv()
                project(k - 1)
        passed[chunks - 1].wait_recv()
        project(chunks - 1)
        sent = [copy for pair in direct for copy in pair] + passed
    else:
        sent = [block_copy(tok_ref, mine, peer, way, k) for k in range(chunks) for way, peer in enumerate(peers)]
        for copy in sent:
            copy.start()
        own_copy.wait()
        for k in range(chunks):
            for way in range(n_tp - 1):
                sent[k * (n_tp - 1) + way].wait_recv()
            project(k)

    for g in range(key_heads):
        border_out[:, g * four : (g + 1) * four] = ext[
            8 + length - BORDER : 8 + length, g * six : g * six + four
        ].astype(BF16)
    border_copy = pltpu.make_async_remote_copy(
        src_ref=border_out, dst_ref=border_in, send_sem=border_sem.at[0], recv_sem=border_sem.at[1],
        device_id={"ctx": lax.rem(ctx + 1, n_ctx)}, device_id_type=MESH,
    )

    @pl.when(ctx < n_ctx - 1)
    def _():
        border_copy.start()

    for copy in small_copies:
        copy.wait()
    mixers = mm_rows(gath[...], wm[...]).astype(BF16).astype(F32)
    columns = mixers.shape[1]
    lane = lax.broadcasted_iota(jnp.int32, (1, columns), 1)
    rate = jnp.zeros((1, columns), F32)
    bias = jnp.zeros((1, columns), F32)
    for h in range(heads):
        here = lane == 4 * (h // 2) + 2 + h % 2
        rate = jnp.where(here, dl_ref[h], rate)
        bias = jnp.where(here, sb_ref[h], bias)
    strength = sigmoid(mixers)
    log_decay = jnp.maximum(-jnp.exp(rate) * softplus(mixers + bias), LEAST_LOG)
    at_row = lax.broadcasted_iota(jnp.int32, (length, length), 0)
    at_col = lax.broadcasted_iota(jnp.int32, (length, length), 1)
    lower = jnp.where(at_row >= at_col, 1.0, 0.0)
    cumulative = jnp.dot(lower, log_decay, precision=TOP_PRECISION, preferred_element_type=F32)

    ext[0:8, :] = jnp.zeros((8, ext.shape[1]), F32)

    def convolve(count):
        def one(g, carry):
            for t in range(4):
                place = pl.ds(pl.multiple_of(g * six + t * WIDTH, WIDTH), WIDTH)
                taps = cw_ref[g, :, t * WIDTH : (t + 1) * WIDTH].astype(F32)
                total = taps[0:1] * ext[5 : 5 + count, place]
                for j in range(1, 4):
                    total = total + taps[j : j + 1] * ext[5 + j : 5 + j + count, place]
                target = pl.ds(pl.multiple_of(g * four + t * WIDTH, WIDTH), WIDTH)
                act[0:count, target] = (total * sigmoid(total)).astype(BF16)
            return carry

        lax.fori_loop(0, key_heads, one, 0)

    convolve(length)

    @pl.when(ctx > 0)
    def _():
        border_copy.wait_recv()
        for g in range(key_heads):
            ext[0:8, g * six : g * six + four] = border_in[BORDER - 8 : BORDER, g * four : (g + 1) * four].astype(F32)
        convolve(BORDER)

    wide = lax.broadcasted_iota(jnp.int32, (length, WIDTH), 1)
    for g in range(key_heads):
        query = act[:, g * four : g * four + WIDTH].astype(F32)
        key = act[:, g * four + WIDTH : g * four + 2 * WIDTH].astype(F32)
        query_unit = lax.rsqrt(jnp.sum(query * query, axis=1, keepdims=True) + EPSILON)
        key_unit = lax.rsqrt(jnp.sum(key * key, axis=1, keepdims=True) + EPSILON)
        for r in range(2):
            h = 2 * g + r
            cum = cumulative[:, 4 * g + 2 + r : 4 * g + 3 + r]
            beta = strength[:, 4 * g + r : 4 * g + r + 1]
            packed = jnp.where(
                wide == 0, cum, jnp.where(wide == 1, beta, jnp.where(wide == 2, key_unit, query_unit))
            )
            col[h] = packed
            row[h] = jnp.transpose(packed)[0:8]

    def heads_of(step, carry):
        i = lax.broadcasted_iota(jnp.int32, (length, length), 0)
        j = lax.broadcasted_iota(jnp.int32, (length, length), 1)
        apart = jnp.bitwise_xor(i, j)
        lows, inverses = [], []
        for b in range(batch):
            g = step * batch + b
            key = act[:, pl.ds(pl.multiple_of(g * four + WIDTH, WIDTH), WIDTH)]
            key_key = mm_rows(key, key)
            for r in range(2):
                h = 2 * g + r
                scal, across = col[h], row[h]
                cum, beta, key_unit = (scal[:, n : n + 1] for n in range(3))
                within = jnp.where(i >= j, jnp.exp(jnp.where(i >= j, cum - across[0:1], 0.0)), 0.0) * across[2:3]
                low = jnp.where(i > j, within * key_key * (beta * key_unit), 0.0).astype(BF16)
                lows.append(low)
                inverses.append(jnp.where(i == j, 1.0, jnp.where(apart == 1, -low.astype(F32), 0.0)).astype(BF16))
        span = 2
        while span < length:
            between = (apart >= span) & (apart < 2 * span)
            firsts = [
                mm(t, jnp.where(between, low.astype(F32), 0.0).astype(BF16)).astype(BF16)
                for t, low in zip(inverses, lows)
            ]
            inverses = [t - mm(first, t).astype(BF16) for t, first in zip(inverses, firsts)]
            span *= 2
        for n, inverse in enumerate(inverses):
            g = step * batch + n // 2
            r = n % 2
            h = 2 * g + r
            scal = col[h]
            cum, beta, key_unit = (scal[:, m : m + 1] for m in range(3))
            key = act[:, pl.ds(pl.multiple_of(g * four + WIDTH, WIDTH), WIDTH)].astype(F32)
            vector = act[:, pl.ds(pl.multiple_of(g * four + (2 + r) * WIDTH, WIDTH), WIDTH)].astype(F32)
            last = cum[length - 1 : length]
            right = jnp.concatenate([vector * beta, key * (beta * jnp.exp(cum) * key_unit)], axis=1).astype(BF16)
            solved = mm(inverse, right).astype(BF16)
            solutions[h] = solved
            tail = (key * (jnp.exp(last - cum) * key_unit)).astype(BF16)
            ends = mm_over_rows(tail, solved)
            inject[h] = ends[:, :WIDTH]
            minus[h] = ends[:, WIDTH:].astype(BF16)
            decay_all[h] = jnp.broadcast_to(jnp.exp(last), (8, WIDTH))
        return carry

    lax.fori_loop(0, key_heads // batch, heads_of, 0)

    def state_copy(h):
        return pltpu.make_async_remote_copy(
            src_ref=s_out.at[h], dst_ref=s_in.at[h], send_sem=state_send.at[h], recv_sem=state_recv.at[h],
            device_id={"ctx": lax.rem(ctx + 1, n_ctx)}, device_id_type=MESH,
        )

    def within_block(g, carry):
        i = lax.broadcasted_iota(jnp.int32, (length, length), 0)
        j = lax.broadcasted_iota(jnp.int32, (length, length), 1)
        query = act[:, pl.ds(pl.multiple_of(g * four, WIDTH), WIDTH)]
        key = act[:, pl.ds(pl.multiple_of(g * four + WIDTH, WIDTH), WIDTH)]
        query_key = mm_rows(query, key)
        for r in range(2):
            h = 2 * g + r
            scal, across = col[h], row[h]
            cum, query_unit = scal[:, 0:1], scal[:, 3:4]
            within = jnp.where(i >= j, jnp.exp(jnp.where(i >= j, cum - across[0:1], 0.0)), 0.0) * across[2:3]
            local = mm((within * query_key * query_unit).astype(BF16), solutions[h])
            own[h] = local[:, :WIDTH]
            reach[h] = (query.astype(F32) * (jnp.exp(cum) * query_unit) - local[:, WIDTH:]).astype(BF16)
        return carry

    def finish(h):
        core = (own[h] + mm(reach[h], s_in[h])).astype(BF16).astype(F32)
        gated = ext[8 : 8 + length, pl.ds(pl.multiple_of((h // 2) * six + four + (h % 2) * WIDTH, WIDTH), WIDTH)]
        scaled = core * lax.rsqrt(jnp.mean(core * core, axis=1, keepdims=True) + EPSILON)
        normed[:, pl.ds(pl.multiple_of(h * WIDTH, WIDTH), WIDTH)] = (
            gain_ref[...] * scaled * (gated * sigmoid(gated))
        ).astype(BF16)

    early = ctx < n_ctx // 2 - 1

    @pl.when(jnp.logical_not(early))
    def _():
        lax.fori_loop(0, key_heads, within_block, 0)

    for h in range(heads):
        @pl.when(ctx > 0)
        def _():
            state_copy(h).wait_recv()

        @pl.when(ctx == 0)
        def _():
            s_in[h] = jnp.zeros((WIDTH, WIDTH), BF16)

        @pl.when(ctx < n_ctx - 1)
        def _():
            before = s_in[h]
            after = decay_all[h, 0:1, :] * before.astype(F32) - mm(minus[h], before) + inject[h]
            s_out[h] = after.astype(BF16)
            state_copy(h).start()

        @pl.when(ctx == n_ctx - 1)
        def _():
            finish(h)

    @pl.when(early)
    def _():
        lax.fori_loop(0, key_heads, within_block, 0)

    @pl.when(ctx < n_ctx - 1)
    def _():
        def one(h, carry):
            finish(h)
            return carry

        lax.fori_loop(0, heads, one, 0)

    wo_copy.wait()
    pieces = rs_send.shape[0]
    piece = depth // pieces

    def share_copy(q, k):
        peer = lax.rem(tp + k + 1, n_tp)
        place = pl.ds(q * piece, piece)
        return pltpu.make_async_remote_copy(
            src_ref=stage.at[pl.ds(pl.multiple_of(peer * rows, 16), rows), place],
            dst_ref=landed.at[k, :, place],
            send_sem=rs_send.at[q, k], recv_sem=rs_recv.at[q, k],
            device_id={"tp": peer}, device_id_type=MESH,
        )

    for q in range(pieces):
        for t in range(0, piece, 256):
            place = slice(q * piece + t, q * piece + t + 256)
            stage[:, place] = mm(normed[...], wo[:, place]).astype(BF16)
        for k in range(n_tp - 1):
            share_copy(q, k).start()
    for q in range(pieces):
        place = slice(q * piece, (q + 1) * piece)
        total = stage[mine, place].astype(F32)
        for k in range(n_tp - 1):
            share_copy(q, k).wait_recv()
            total = total + landed[k, :, place].astype(F32)
        out_ref[:, place] = total.astype(BF16)
    for q in range(pieces):
        for k in range(n_tp - 1):
            share_copy(q, k).wait_send()
    for copy in sent:
        copy.wait_send()

    @pl.when(ctx < n_ctx - 1)
    def _():
        border_copy.wait_send()
        for h in range(heads):
            state_copy(h).wait_send()


def on_device(tokens, w_project, w_mixers, conv_weight, decay_log, step_bias, norm_gain, w_output):
    n_ctx, n_tp = lax.axis_size("ctx"), lax.axis_size("tp")
    rows, depth = tokens.shape
    length = rows * n_tp
    key_heads = conv_weight.shape[0]
    heads = 2 * key_heads
    inner = heads * WIDTH
    batch = 2 if key_heads % 2 == 0 else 1
    pieces = 4
    chunks = 4
    ways = 3 if n_tp == 4 else n_tp - 1
    vmem = pl.BlockSpec(memory_space=pltpu.VMEM)
    far = pl.BlockSpec(memory_space=pl.ANY)
    dma = pltpu.SemaphoreType.DMA
    square = (heads, WIDTH, WIDTH)
    return pl.pallas_call(
        functools.partial(kernel, n_ctx, n_tp, key_heads, batch, chunks),
        out_shape=jax.ShapeDtypeStruct((rows, depth), BF16),
        in_specs=[far] * 8,
        out_specs=vmem,
        scratch_shapes=[
            pltpu.VMEM((length, depth), BF16),
            pltpu.VMEM(w_project.shape, BF16),
            pltpu.VMEM((w_mixers.shape[1], depth), BF16),
            pltpu.VMEM(w_output.shape, BF16),
            pltpu.VMEM(conv_weight.shape, BF16),
            pltpu.SMEM((heads,), F32),
            pltpu.SMEM((heads,), F32),
            pltpu.VMEM((1, WIDTH), F32),
            pltpu.VMEM((8 + length, key_heads * 6 * WIDTH), F32),
            pltpu.VMEM((length, key_heads * 4 * WIDTH), BF16),
            pltpu.VMEM((BORDER, key_heads * 4 * WIDTH), BF16),
            pltpu.VMEM((BORDER, key_heads * 4 * WIDTH), BF16),
            pltpu.VMEM((heads, length, WIDTH), F32),
            pltpu.VMEM((heads, 8, length), F32),
            pltpu.VMEM((heads, length, 2 * WIDTH), BF16),
            pltpu.VMEM(square, BF16),
            pltpu.VMEM(square, F32),
            pltpu.VMEM((heads, length, WIDTH), F32),
            pltpu.VMEM((heads, length, WIDTH), BF16),
            pltpu.VMEM(square, BF16),
            pltpu.VMEM(square, BF16),
            pltpu.VMEM((heads, 8, WIDTH), F32),
            pltpu.VMEM((length, inner), BF16),
            pltpu.VMEM((length, depth), BF16),
            pltpu.VMEM((n_tp - 1, rows, depth), BF16),
            dma, dma((chunks,)), dma((5,)), dma,
            dma((ways, chunks)), dma((ways, chunks)), dma((2,)),
            dma((heads,)), dma((heads,)),
            dma((pieces, n_tp - 1)), dma((pieces, n_tp - 1)),
        ],
        compiler_params=pltpu.CompilerParams(
            collective_id=0, has_side_effects=True, vmem_limit_bytes=63 * 1024 * 1024
        ),
    )(
        tokens, w_project, w_mixers.T, conv_weight, decay_log, step_bias, norm_gain.reshape(1, WIDTH), w_output,
    )


def solution(mesh):
    placed = (
        P(("ctx", "tp"), None),
        P(None, "tp"),
        P(None, "tp"),
        P("tp", None, None),
        P("tp"),
        P("tp"),
        P(),
        P("tp", None),
    )
    return jax.shard_map(
        on_device, mesh=mesh, in_specs=placed, out_specs=P(("ctx", "tp"), None), check_vma=False
    )
```

```python
import functools

import jax
import jax.numpy as jnp
from jax import lax
from jax.experimental import pallas as pl
from jax.experimental.pallas import tpu as pltpu
from jax.sharding import PartitionSpec as P

EPSILON = 1e-06
TOP_PRECISION = lax.Precision.HIGHEST
MESH = pl.DeviceIdType.MESH
WIDTH = 128
F32 = jnp.float32
BF16 = jnp.bfloat16
BORDER = 16
LEAST_LOG = -120.0


def mm(a, b):
    return jnp.dot(a, b, preferred_element_type=F32)


def mm_rows(a, b):
    return lax.dot_general(a, b, (((1,), (1,)), ((), ())), preferred_element_type=F32)


def mm_over_rows(a, b):
    return lax.dot_general(a, b, (((0,), (0,)), ((), ())), preferred_element_type=F32)


def sigmoid(x):
    return 1.0 / (1.0 + jnp.exp(-x))


def softplus(x):
    small = jnp.exp(-jnp.abs(x))
    grown = 1.0 + small
    tail = jnp.where(grown == 1.0, small, jnp.log(grown) * small / jnp.where(grown == 1.0, 1.0, grown - 1.0))
    return jnp.maximum(x, 0.0) + tail


def kernel(
    n_ctx, n_tp, key_heads, batch, chunks,
    tok_ref, wp_ref, wm_ref, cw_in, dl_in, sb_in, gain_in, wo_ref,
    out_ref,
    gath, wp, wm, wo, cw_ref, dl_ref, sb_ref, gain_ref,
    ext, act, border_out, border_in, col, row, solutions, minus, inject, own, reach,
    s_in, s_out, decay_all, normed, stage, landed,
    own_sem, wp_sem, small_sem, wo_sem, ag_send, ag_recv, border_sem, state_send, state_recv, rs_send, rs_recv,
):
    rows = tok_ref.shape[0]
    length = rows * n_tp
    heads = 2 * key_heads
    depth = wo_ref.shape[1]
    ctx, tp = lax.axis_index("ctx"), lax.axis_index("tp")
    six, four = 6 * WIDTH, 4 * WIDTH

    k_rows = depth // chunks
    small_copies = [
        pltpu.make_async_copy(source, target, small_sem.at[n])
        for n, (source, target) in enumerate(
            [(wm_ref, wm), (cw_in, cw_ref), (dl_in, dl_ref), (sb_in, sb_ref), (gain_in, gain_ref)]
        )
    ]
    wo_copy = pltpu.make_async_copy(wo_ref, wo, wo_sem)
    wp_copies = [
        pltpu.make_async_copy(wp_ref.at[pl.ds(k * k_rows, k_rows)], wp.at[pl.ds(k * k_rows, k_rows)], wp_sem.at[k])
        for k in range(chunks)
    ]
    mine = pl.ds(pl.multiple_of(tp * rows, 16), rows)
    own_copy = pltpu.make_async_copy(tok_ref, gath.at[mine], own_sem)
    own_copy.start()
    for copy in wp_copies[: chunks // 2]:
        copy.start()

    barrier = pltpu.get_barrier_semaphore()
    peers = [lax.rem(tp + k, n_tp) for k in range(1, n_tp)]
    for peer in peers:
        pl.semaphore_signal(barrier, inc=1, device_id={"tp": peer}, device_id_type=MESH)

    @pl.when(ctx > 0)
    def _():
        pl.semaphore_signal(barrier, inc=1, device_id={"ctx": ctx - 1}, device_id_type=MESH)

    @pl.when(ctx < n_ctx - 1)
    def _():
        pl.semaphore_signal(barrier, inc=1, device_id={"ctx": ctx + 1}, device_id_type=MESH)

    beside = jnp.where(ctx > 0, 1, 0) + jnp.where(ctx < n_ctx - 1, 1, 0)
    pl.semaphore_wait(barrier, n_tp - 1 + beside)

    def block_copy(source, held, peer, way, k):
        place = pl.ds(k * k_rows, k_rows)
        return pltpu.make_async_remote_copy(
            src_ref=source.at[:, place] if held is mine else source.at[held, place],
            dst_ref=gath.at[held, place],
            send_sem=ag_send.at[way, k], recv_sem=ag_recv.at[way, k],
            device_id={"tp": peer}, device_id_type=MESH,
        )

    def project(half):
        groups = chunks // 2
        for k in range(half * groups, (half + 1) * groups):
            wp_copies[k].wait()
        place = slice(half * groups * k_rows, (half + 1) * groups * k_rows)
        total_columns = key_heads * six
        for start in range(0, total_columns, 256):
            span = slice(start, start + 256)
            part = mm(gath[:, place], wp[place, span])
            if half == 1:
                part = (part + ext[8 : 8 + length, span]).astype(BF16).astype(F32)
            ext[8 : 8 + length, span] = part

    def start_rest():
        for copy in wp_copies[chunks // 2 :]:
            copy.start()
        for copy in small_copies:
            copy.start()
        wo_copy.start()

    if n_tp == 4:
        x_peer = tp + 1 - 2 * lax.rem(tp, 2)
        y_peer = lax.rem(tp + 2, 4)
        x_rows = pl.ds(pl.multiple_of(x_peer * rows, 16), rows)
        y_rows = pl.ds(pl.multiple_of(y_peer * rows, 16), rows)
        direct = [
            [block_copy(tok_ref, mine, peer, way, k) for way, peer in enumerate((x_peer, y_peer))]
            for k in range(chunks)
        ]
        passed = [
            block_copy(gath, x_rows, y_peer, 2, k) if k % 2 == 0 else block_copy(gath, y_rows, x_peer, 2, k)
            for k in range(chunks)
        ]
        for pair in direct:
            for copy in pair:
                copy.start()
        start_rest()
        own_copy.wait()
        for k in range(chunks):
            for copy in direct[k]:
                copy.wait_recv()
            passed[k].start()
            if k == chunks - 1:
                for early_copy in passed[: chunks // 2]:
                    early_copy.wait_recv()
                project(0)
        for late_copy in passed[chunks // 2 :]:
            late_copy.wait_recv()
        project(1)
        sent = [copy for pair in direct for copy in pair] + passed
    else:
        sent = [block_copy(tok_ref, mine, peer, way, k) for k in range(chunks) for way, peer in enumerate(peers)]
        for copy in sent:
            copy.start()
        start_rest()
        own_copy.wait()
        for k in range(chunks):
            for way in range(n_tp - 1):
                sent[k * (n_tp - 1) + way].wait_recv()
            if (k + 1) % (chunks // 2) == 0:
                project((k + 1) // (chunks // 2) - 1)

    for g in range(key_heads):
        border_out[:, g * four : (g + 1) * four] = ext[
            8 + length - BORDER : 8 + length, g * six : g * six + four
        ].astype(BF16)
    border_copy = pltpu.make_async_remote_copy(
        src_ref=border_out, dst_ref=border_in, send_sem=border_sem.at[0], recv_sem=border_sem.at[1],
        device_id={"ctx": lax.rem(ctx + 1, n_ctx)}, device_id_type=MESH,
    )

    @pl.when(ctx < n_ctx - 1)
    def _():
        border_copy.start()

    for copy in small_copies:
        copy.wait()
    mixers = mm_rows(gath[...], wm[...]).astype(BF16).astype(F32)
    columns = mixers.shape[1]
    lane = lax.broadcasted_iota(jnp.int32, (1, columns), 1)
    rate = jnp.zeros((1, columns), F32)
    bias = jnp.zeros((1, columns), F32)
    for h in range(heads):
        here = lane == 4 * (h // 2) + 2 + h % 2
        rate = jnp.where(here, dl_ref[h], rate)
        bias = jnp.where(here, sb_ref[h], bias)
    strength = sigmoid(mixers)
    log_decay = jnp.maximum(-jnp.exp(rate) * softplus(mixers + bias), LEAST_LOG)
    at_row = lax.broadcasted_iota(jnp.int32, (length, length), 0)
    at_col = lax.broadcasted_iota(jnp.int32, (length, length), 1)
    lower = jnp.where(at_row >= at_col, 1.0, 0.0)
    cumulative = jnp.dot(lower, log_decay, precision=TOP_PRECISION, preferred_element_type=F32)

    ext[0:8, :] = jnp.zeros((8, ext.shape[1]), F32)

    def convolve(count):
        def one(g, carry):
            for t in range(4):
                place = pl.ds(pl.multiple_of(g * six + t * WIDTH, WIDTH), WIDTH)
                taps = cw_ref[g, :, t * WIDTH : (t + 1) * WIDTH].astype(F32)
                total = taps[0:1] * ext[5 : 5 + count, place]
                for j in range(1, 4):
                    total = total + taps[j : j + 1] * ext[5 + j : 5 + j + count, place]
                target = pl.ds(pl.multiple_of(g * four + t * WIDTH, WIDTH), WIDTH)
                act[0:count, target] = (total * sigmoid(total)).astype(BF16)
            return carry

        lax.fori_loop(0, key_heads, one, 0)

    convolve(length)

    @pl.when(ctx > 0)
    def _():
        border_copy.wait_recv()
        for g in range(key_heads):
            ext[0:8, g * six : g * six + four] = border_in[BORDER - 8 : BORDER, g * four : (g + 1) * four].astype(F32)
        convolve(BORDER)

    wide = lax.broadcasted_iota(jnp.int32, (length, WIDTH), 1)
    for g in range(key_heads):
        query = act[:, g * four : g * four + WIDTH].astype(F32)
        key = act[:, g * four + WIDTH : g * four + 2 * WIDTH].astype(F32)
        query_unit = lax.rsqrt(jnp.sum(query * query, axis=1, keepdims=True) + EPSILON)
        key_unit = lax.rsqrt(jnp.sum(key * key, axis=1, keepdims=True) + EPSILON)
        for r in range(2):
            h = 2 * g + r
            cum = cumulative[:, 4 * g + 2 + r : 4 * g + 3 + r]
            beta = strength[:, 4 * g + r : 4 * g + r + 1]
            packed = jnp.where(
                wide == 0, cum, jnp.where(wide == 1, beta, jnp.where(wide == 2, key_unit, query_unit))
            )
            col[h] = packed
            row[h] = jnp.transpose(packed)[0:8]

    def heads_of(step, carry):
        i = lax.broadcasted_iota(jnp.int32, (length, length), 0)
        j = lax.broadcasted_iota(jnp.int32, (length, length), 1)
        apart = jnp.bitwise_xor(i, j)
        lows, inverses = [], []
        for b in range(batch):
            g = step * batch + b
            key = act[:, pl.ds(pl.multiple_of(g * four + WIDTH, WIDTH), WIDTH)]
            key_key = mm_rows(key, key)
            for r in range(2):
                h = 2 * g + r
                scal, across = col[h], row[h]
                cum, beta, key_unit = (scal[:, n : n + 1] for n in range(3))
                within = jnp.where(i >= j, jnp.exp(jnp.where(i >= j, cum - across[0:1], 0.0)), 0.0) * across[2:3]
                low = jnp.where(i > j, within * key_key * (beta * key_unit), 0.0).astype(BF16)
                lows.append(low)
                inverses.append(jnp.where(i == j, 1.0, jnp.where(apart == 1, -low.astype(F32), 0.0)).astype(BF16))
        span = 2
        while span < length:
            between = (apart >= span) & (apart < 2 * span)
            firsts = [
                mm(t, jnp.where(between, low.astype(F32), 0.0).astype(BF16)).astype(BF16)
                for t, low in zip(inverses, lows)
            ]
            inverses = [t - mm(first, t).astype(BF16) for t, first in zip(inverses, firsts)]
            span *= 2
        for n, inverse in enumerate(inverses):
            g = step * batch + n // 2
            r = n % 2
            h = 2 * g + r
            scal = col[h]
            cum, beta, key_unit = (scal[:, m : m + 1] for m in range(3))
            key = act[:, pl.ds(pl.multiple_of(g * four + WIDTH, WIDTH), WIDTH)].astype(F32)
            vector = act[:, pl.ds(pl.multiple_of(g * four + (2 + r) * WIDTH, WIDTH), WIDTH)].astype(F32)
            last = cum[length - 1 : length]
            right = jnp.concatenate([vector * beta, key * (beta * jnp.exp(cum) * key_unit)], axis=1).astype(BF16)
            solved = mm(inverse, right).astype(BF16)
            solutions[h] = solved
            tail = (key * (jnp.exp(last - cum) * key_unit)).astype(BF16)
            ends = mm_over_rows(tail, solved)
            inject[h] = ends[:, :WIDTH]
            minus[h] = ends[:, WIDTH:].astype(BF16)
            decay_all[h] = jnp.broadcast_to(jnp.exp(last), (8, WIDTH))
        return carry

    lax.fori_loop(0, key_heads // batch, heads_of, 0)

    def state_copy(h):
        return pltpu.make_async_remote_copy(
            src_ref=s_out.at[h], dst_ref=s_in.at[h], send_sem=state_send.at[h], recv_sem=state_recv.at[h],
            device_id={"ctx": lax.rem(ctx + 1, n_ctx)}, device_id_type=MESH,
        )

    def within_block(g, carry):
        i = lax.broadcasted_iota(jnp.int32, (length, length), 0)
        j = lax.broadcasted_iota(jnp.int32, (length, length), 1)
        query = act[:, pl.ds(pl.multiple_of(g * four, WIDTH), WIDTH)]
        key = act[:, pl.ds(pl.multiple_of(g * four + WIDTH, WIDTH), WIDTH)]
        query_key = mm_rows(query, key)
        for r in range(2):
            h = 2 * g + r
            scal, across = col[h], row[h]
            cum, query_unit = scal[:, 0:1], scal[:, 3:4]
            within = jnp.where(i >= j, jnp.exp(jnp.where(i >= j, cum - across[0:1], 0.0)), 0.0) * across[2:3]
            local = mm((within * query_key * query_unit).astype(BF16), solutions[h])
            own[h] = local[:, :WIDTH]
            reach[h] = (query.astype(F32) * (jnp.exp(cum) * query_unit) - local[:, WIDTH:]).astype(BF16)
        return carry

    def finish(h):
        core = (own[h] + mm(reach[h], s_in[h])).astype(BF16).astype(F32)
        gated = ext[8 : 8 + length, pl.ds(pl.multiple_of((h // 2) * six + four + (h % 2) * WIDTH, WIDTH), WIDTH)]
        scaled = core * lax.rsqrt(jnp.mean(core * core, axis=1, keepdims=True) + EPSILON)
        normed[:, pl.ds(pl.multiple_of(h * WIDTH, WIDTH), WIDTH)] = (
            gain_ref[...] * scaled * (gated * sigmoid(gated))
        ).astype(BF16)

    early = ctx < n_ctx // 2 - 1

    @pl.when(jnp.logical_not(early))
    def _():
        lax.fori_loop(0, key_heads, within_block, 0)

    for h in range(heads):
        @pl.when(ctx > 0)
        def _():
            state_copy(h).wait_recv()

        @pl.when(ctx == 0)
        def _():
            s_in[h] = jnp.zeros((WIDTH, WIDTH), BF16)

        @pl.when(ctx < n_ctx - 1)
        def _():
            before = s_in[h]
            after = decay_all[h, 0:1, :] * before.astype(F32) - mm(minus[h], before) + inject[h]
            s_out[h] = after.astype(BF16)
            state_copy(h).start()

        @pl.when(ctx == n_ctx - 1)
        def _():
            finish(h)

    @pl.when(early)
    def _():
        lax.fori_loop(0, key_heads, within_block, 0)

    @pl.when(ctx < n_ctx - 1)
    def _():
        def one(h, carry):
            finish(h)
            return carry

        lax.fori_loop(0, heads, one, 0)

    wo_copy.wait()
    pieces = rs_send.shape[0]
    piece = depth // pieces

    def share_copy(q, k):
        peer = lax.rem(tp + k + 1, n_tp)
        place = pl.ds(q * piece, piece)
        return pltpu.make_async_remote_copy(
            src_ref=stage.at[pl.ds(pl.multiple_of(peer * rows, 16), rows), place],
            dst_ref=landed.at[k, :, place],
            send_sem=rs_send.at[q, k], recv_sem=rs_recv.at[q, k],
            device_id={"tp": peer}, device_id_type=MESH,
        )

    for q in range(pieces):
        for t in range(0, piece, 256):
            place = slice(q * piece + t, q * piece + t + 256)
            stage[:, place] = mm(normed[...], wo[:, place]).astype(BF16)
        for k in range(n_tp - 1):
            share_copy(q, k).start()
    for q in range(pieces):
        place = slice(q * piece, (q + 1) * piece)
        total = stage[mine, place].astype(F32)
        for k in range(n_tp - 1):
            share_copy(q, k).wait_recv()
            total = total + landed[k, :, place].astype(F32)
        out_ref[:, place] = total.astype(BF16)
    for q in range(pieces):
        for k in range(n_tp - 1):
            share_copy(q, k).wait_send()
    for copy in sent:
        copy.wait_send()

    @pl.when(ctx < n_ctx - 1)
    def _():
        border_copy.wait_send()
        for h in range(heads):
            state_copy(h).wait_send()


def on_device(tokens, w_project, w_mixers, conv_weight, decay_log, step_bias, norm_gain, w_output):
    n_ctx, n_tp = lax.axis_size("ctx"), lax.axis_size("tp")
    rows, depth = tokens.shape
    length = rows * n_tp
    key_heads = conv_weight.shape[0]
    heads = 2 * key_heads
    inner = heads * WIDTH
    batch = next(n for n in (4, 2, 1) if key_heads % n == 0)
    pieces = 4
    chunks = 4
    ways = 3 if n_tp == 4 else n_tp - 1
    vmem = pl.BlockSpec(memory_space=pltpu.VMEM)
    far = pl.BlockSpec(memory_space=pltpu.HBM)
    dma = pltpu.SemaphoreType.DMA
    square = (heads, WIDTH, WIDTH)
    return pl.pallas_call(
        functools.partial(kernel, n_ctx, n_tp, key_heads, batch, chunks),
        out_shape=jax.ShapeDtypeStruct((rows, depth), BF16),
        in_specs=[far] * 8,
        out_specs=vmem,
        scratch_shapes=[
            pltpu.VMEM((length, depth), BF16),
            pltpu.VMEM(w_project.shape, BF16),
            pltpu.VMEM((w_mixers.shape[1], depth), BF16),
            pltpu.VMEM(w_output.shape, BF16),
            pltpu.VMEM(conv_weight.shape, BF16),
            pltpu.SMEM((heads,), F32),
            pltpu.SMEM((heads,), F32),
            pltpu.VMEM((1, WIDTH), F32),
            pltpu.VMEM((8 + length, key_heads * 6 * WIDTH), F32),
            pltpu.VMEM((length, key_heads * 4 * WIDTH), BF16),
            pltpu.VMEM((BORDER, key_heads * 4 * WIDTH), BF16),
            pltpu.VMEM((BORDER, key_heads * 4 * WIDTH), BF16),
            pltpu.VMEM((heads, length, WIDTH), F32),
            pltpu.VMEM((heads, 8, length), F32),
            pltpu.VMEM((heads, length, 2 * WIDTH), BF16),
            pltpu.VMEM(square, BF16),
            pltpu.VMEM(square, F32),
            pltpu.VMEM((heads, length, WIDTH), F32),
            pltpu.VMEM((heads, length, WIDTH), BF16),
            pltpu.VMEM(square, BF16),
            pltpu.VMEM(square, BF16),
            pltpu.VMEM((heads, 8, WIDTH), F32),
            pltpu.VMEM((length, inner), BF16),
            pltpu.VMEM((length, depth), BF16),
            pltpu.VMEM((n_tp - 1, rows, depth), BF16),
            dma, dma((chunks,)), dma((5,)), dma,
            dma((ways, chunks)), dma((ways, chunks)), dma((2,)),
            dma((heads,)), dma((heads,)),
            dma((pieces, n_tp - 1)), dma((pieces, n_tp - 1)),
        ],
        compiler_params=pltpu.CompilerParams(
            collective_id=0, has_side_effects=True, vmem_limit_bytes=52 * 1024 * 1024
        ),
    )(
        tokens, w_project, w_mixers.T, conv_weight, decay_log, step_bias, norm_gain.reshape(1, WIDTH), w_output,
    )


def solution(mesh):
    placed = (
        P(("ctx", "tp"), None),
        P(None, "tp"),
        P(None, "tp"),
        P("tp", None, None),
        P("tp"),
        P("tp"),
        P(),
        P("tp", None),
    )
    return jax.shard_map(
        on_device, mesh=mesh, in_specs=placed, out_specs=P(("ctx", "tp"), None), check_vma=False
    )
```

```python
import functools

import jax
import jax.numpy as jnp
from jax import lax
from jax.experimental import pallas as pl
from jax.experimental.pallas import tpu as pltpu
from jax.sharding import PartitionSpec as P

EPSILON = 1e-06
TOP_PRECISION = lax.Precision.HIGHEST
MESH = pl.DeviceIdType.MESH
WIDTH = 128
F32 = jnp.float32
BF16 = jnp.bfloat16
BORDER = 16
LEAST_LOG = -120.0


def mm(a, b):
    return jnp.dot(a, b, preferred_element_type=F32)


def mm_rows(a, b):
    return lax.dot_general(a, b, (((1,), (1,)), ((), ())), preferred_element_type=F32)


def mm_over_rows(a, b):
    return lax.dot_general(a, b, (((0,), (0,)), ((), ())), preferred_element_type=F32)


def sigmoid(x):
    return 1.0 / (1.0 + jnp.exp(-x))


def softplus(x):
    small = jnp.exp(-jnp.abs(x))
    grown = 1.0 + small
    tail = jnp.where(grown == 1.0, small, jnp.log(grown) * small / jnp.where(grown == 1.0, 1.0, grown - 1.0))
    return jnp.maximum(x, 0.0) + tail


def kernel(
    n_ctx, n_tp, key_heads, batch, chunks,
    tok_ref, wp_ref, wm_ref, cw_in, dl_in, sb_in, gain_in, wo_ref,
    out_ref,
    gath, wp, wm, wo, cw_ref, dl_ref, sb_ref, gain_ref,
    ext, act, border_out, border_in, col, row, solutions, minus, inject, own, reach,
    s_in, s_out, decay_all, normed, stage, landed,
    own_sem, wp_sem, small_sem, wo_sem, ag_send, ag_recv, border_sem, state_send, state_recv, rs_send, rs_recv,
):
    rows = tok_ref.shape[0]
    length = rows * n_tp
    heads = 2 * key_heads
    depth = wo_ref.shape[1]
    ctx, tp = lax.axis_index("ctx"), lax.axis_index("tp")
    six, four = 6 * WIDTH, 4 * WIDTH

    k_rows = depth // chunks
    small_copies = [
        pltpu.make_async_copy(source, target, small_sem.at[n])
        for n, (source, target) in enumerate(
            [(wm_ref, wm), (cw_in, cw_ref), (dl_in, dl_ref), (sb_in, sb_ref), (gain_in, gain_ref)]
        )
    ]
    wo_copy = pltpu.make_async_copy(wo_ref, wo, wo_sem)
    wp_copies = [
        pltpu.make_async_copy(wp_ref.at[pl.ds(k * k_rows, k_rows)], wp.at[pl.ds(k * k_rows, k_rows)], wp_sem.at[k])
        for k in range(chunks)
    ]
    mine = pl.ds(pl.multiple_of(tp * rows, 16), rows)
    own_copy = pltpu.make_async_copy(tok_ref, gath.at[mine], own_sem)
    own_copy.start()
    for copy in wp_copies[: chunks // 2]:
        copy.start()

    barrier = pltpu.get_barrier_semaphore()
    peers = [lax.rem(tp + k, n_tp) for k in range(1, n_tp)]
    for peer in peers:
        pl.semaphore_signal(barrier, inc=1, device_id={"tp": peer}, device_id_type=MESH)

    @pl.when(ctx > 0)
    def _():
        pl.semaphore_signal(barrier, inc=1, device_id={"ctx": ctx - 1}, device_id_type=MESH)

    @pl.when(ctx < n_ctx - 1)
    def _():
        pl.semaphore_signal(barrier, inc=1, device_id={"ctx": ctx + 1}, device_id_type=MESH)

    beside = jnp.where(ctx > 0, 1, 0) + jnp.where(ctx < n_ctx - 1, 1, 0)
    pl.semaphore_wait(barrier, n_tp - 1 + beside)

    def block_copy(source, held, peer, way, k):
        place = pl.ds(k * k_rows, k_rows)
        return pltpu.make_async_remote_copy(
            src_ref=source.at[:, place] if held is mine else source.at[held, place],
            dst_ref=gath.at[held, place],
            send_sem=ag_send.at[way, k], recv_sem=ag_recv.at[way, k],
            device_id={"tp": peer}, device_id_type=MESH,
        )

    def project(half):
        groups = chunks // 2
        for k in range(half * groups, (half + 1) * groups):
            wp_copies[k].wait()
        place = slice(half * groups * k_rows, (half + 1) * groups * k_rows)
        total_columns = key_heads * six
        for start in range(0, total_columns, 256):
            span = slice(start, start + 256)
            part = mm(gath[:, place], wp[place, span])
            if half == 1:
                part = (part + ext[8 : 8 + length, span]).astype(BF16).astype(F32)
            ext[8 : 8 + length, span] = part

    def start_rest():
        for copy in wp_copies[chunks // 2 :]:
            copy.start()
        for copy in small_copies:
            copy.start()
        wo_copy.start()

    if n_tp == 4:
        x_peer = tp + 1 - 2 * lax.rem(tp, 2)
        y_peer = lax.rem(tp + 2, 4)
        x_rows = pl.ds(pl.multiple_of(x_peer * rows, 16), rows)
        y_rows = pl.ds(pl.multiple_of(y_peer * rows, 16), rows)
        direct = [
            [block_copy(tok_ref, mine, peer, way, k) for way, peer in enumerate((x_peer, y_peer))]
            for k in range(chunks)
        ]
        passed = [
            block_copy(gath, x_rows, y_peer, 2, k) if k % 2 == 0 else block_copy(gath, y_rows, x_peer, 2, k)
            for k in range(chunks)
        ]
        for pair in direct:
            for copy in pair:
                copy.start()
        start_rest()
        own_copy.wait()
        for k in range(chunks):
            for copy in direct[k]:
                copy.wait_recv()
            passed[k].start()
            if k == chunks - 1:
                for early_copy in passed[: chunks // 2]:
                    early_copy.wait_recv()
                project(0)
        for late_copy in passed[chunks // 2 :]:
            late_copy.wait_recv()
        project(1)
        sent = [copy for pair in direct for copy in pair] + passed
    else:
        sent = [block_copy(tok_ref, mine, peer, way, k) for k in range(chunks) for way, peer in enumerate(peers)]
        for copy in sent:
            copy.start()
        start_rest()
        own_copy.wait()
        for k in range(chunks):
            for way in range(n_tp - 1):
                sent[k * (n_tp - 1) + way].wait_recv()
            if (k + 1) % (chunks // 2) == 0:
                project((k + 1) // (chunks // 2) - 1)

    for g in range(key_heads):
        border_out[:, g * four : (g + 1) * four] = ext[
            8 + length - BORDER : 8 + length, g * six : g * six + four
        ].astype(BF16)
    border_copy = pltpu.make_async_remote_copy(
        src_ref=border_out, dst_ref=border_in, send_sem=border_sem.at[0], recv_sem=border_sem.at[1],
        device_id={"ctx": lax.rem(ctx + 1, n_ctx)}, device_id_type=MESH,
    )

    @pl.when(ctx < n_ctx - 1)
    def _():
        border_copy.start()

    for copy in small_copies:
        copy.wait()
    mixers = mm_rows(gath[...], wm[...]).astype(BF16).astype(F32)
    columns = mixers.shape[1]
    lane = lax.broadcasted_iota(jnp.int32, (1, columns), 1)
    rate = jnp.zeros((1, columns), F32)
    bias = jnp.zeros((1, columns), F32)
    for h in range(heads):
        here = lane == 4 * (h // 2) + 2 + h % 2
        rate = jnp.where(here, dl_ref[h], rate)
        bias = jnp.where(here, sb_ref[h], bias)
    strength = sigmoid(mixers)
    log_decay = jnp.maximum(-jnp.exp(rate) * softplus(mixers + bias), LEAST_LOG)
    at_row = lax.broadcasted_iota(jnp.int32, (length, length), 0)
    at_col = lax.broadcasted_iota(jnp.int32, (length, length), 1)
    lower = jnp.where(at_row >= at_col, 1.0, 0.0)
    cumulative = jnp.dot(lower, log_decay, precision=TOP_PRECISION, preferred_element_type=F32)

    ext[0:8, :] = jnp.zeros((8, ext.shape[1]), F32)

    def convolve(count):
        def one(g, carry):
            for t in range(4):
                place = pl.ds(pl.multiple_of(g * six + t * WIDTH, WIDTH), WIDTH)
                taps = cw_ref[g, :, t * WIDTH : (t + 1) * WIDTH].astype(F32)
                total = taps[0:1] * ext[5 : 5 + count, place]
                for j in range(1, 4):
                    total = total + taps[j : j + 1] * ext[5 + j : 5 + j + count, place]
                target = pl.ds(pl.multiple_of(g * four + t * WIDTH, WIDTH), WIDTH)
                act[0:count, target] = (total * sigmoid(total)).astype(BF16)
            return carry

        lax.fori_loop(0, key_heads, one, 0)

    convolve(length)

    @pl.when(ctx > 0)
    def _():
        border_copy.wait_recv()
        for g in range(key_heads):
            ext[0:8, g * six : g * six + four] = border_in[BORDER - 8 : BORDER, g * four : (g + 1) * four].astype(F32)
        convolve(BORDER)

    wide = lax.broadcasted_iota(jnp.int32, (length, WIDTH), 1)
    for g in range(key_heads):
        query = act[:, g * four : g * four + WIDTH].astype(F32)
        key = act[:, g * four + WIDTH : g * four + 2 * WIDTH].astype(F32)
        query_unit = lax.rsqrt(jnp.sum(query * query, axis=1, keepdims=True) + EPSILON)
        key_unit = lax.rsqrt(jnp.sum(key * key, axis=1, keepdims=True) + EPSILON)
        for r in range(2):
            h = 2 * g + r
            cum = cumulative[:, 4 * g + 2 + r : 4 * g + 3 + r]
            beta = strength[:, 4 * g + r : 4 * g + r + 1]
            packed = jnp.where(
                wide == 0, cum, jnp.where(wide == 1, beta, jnp.where(wide == 2, key_unit, query_unit))
            )
            col[h] = packed
            row[h] = jnp.transpose(packed)[0:8]

    def heads_of(step, carry):
        i = lax.broadcasted_iota(jnp.int32, (length, length), 0)
        j = lax.broadcasted_iota(jnp.int32, (length, length), 1)
        apart = jnp.bitwise_xor(i, j)
        lows, inverses = [], []
        for b in range(batch):
            g = step * batch + b
            key = act[:, pl.ds(pl.multiple_of(g * four + WIDTH, WIDTH), WIDTH)]
            key_key = mm_rows(key, key)
            for r in range(2):
                h = 2 * g + r
                scal, across = col[h], row[h]
                cum, beta, key_unit = (scal[:, n : n + 1] for n in range(3))
                within = jnp.exp(jnp.where(i > j, cum - across[0:1], 0.0)) * across[2:3]
                low = jnp.where(i > j, within * key_key * (beta * key_unit), 0.0).astype(BF16)
                lows.append(low)
                inverses.append(jnp.where(i == j, 1.0, jnp.where(apart == 1, -low.astype(F32), 0.0)).astype(BF16))
        span = 2
        while span < length:
            between = jnp.where((apart >= span) & (apart < 2 * span), 1.0, 0.0).astype(BF16)
            firsts = [mm(t, low * between).astype(BF16) for t, low in zip(inverses, lows)]
            inverses = [t - mm(first, t).astype(BF16) for t, first in zip(inverses, firsts)]
            span *= 2
        for n, inverse in enumerate(inverses):
            g = step * batch + n // 2
            r = n % 2
            h = 2 * g + r
            scal = col[h]
            cum, beta, key_unit = (scal[:, m : m + 1] for m in range(3))
            key = act[:, pl.ds(pl.multiple_of(g * four + WIDTH, WIDTH), WIDTH)].astype(F32)
            vector = act[:, pl.ds(pl.multiple_of(g * four + (2 + r) * WIDTH, WIDTH), WIDTH)].astype(F32)
            last = cum[length - 1 : length]
            right = jnp.concatenate([vector * beta, key * (beta * jnp.exp(cum) * key_unit)], axis=1).astype(BF16)
            solved = mm(inverse, right).astype(BF16)
            solutions[h] = solved
            tail = (key * (jnp.exp(last - cum) * key_unit)).astype(BF16)
            ends = mm_over_rows(tail, solved)
            inject[h] = ends[:, :WIDTH]
            minus[h] = ends[:, WIDTH:].astype(BF16)
            decay_all[h] = jnp.broadcast_to(jnp.exp(last), (8, WIDTH))
        return carry

    lax.fori_loop(0, key_heads // batch, heads_of, 0)

    def state_copy(h):
        return pltpu.make_async_remote_copy(
            src_ref=s_out.at[h], dst_ref=s_in.at[h], send_sem=state_send.at[h], recv_sem=state_recv.at[h],
            device_id={"ctx": lax.rem(ctx + 1, n_ctx)}, device_id_type=MESH,
        )

    def gate_place(h):
        return pl.ds(pl.multiple_of((h // 2) * six + four + (h % 2) * WIDTH, WIDTH), WIDTH)

    def within_block(g, carry):
        i = lax.broadcasted_iota(jnp.int32, (length, length), 0)
        j = lax.broadcasted_iota(jnp.int32, (length, length), 1)
        query = act[:, pl.ds(pl.multiple_of(g * four, WIDTH), WIDTH)]
        key = act[:, pl.ds(pl.multiple_of(g * four + WIDTH, WIDTH), WIDTH)]
        query_key = mm_rows(query, key)
        for r in range(2):
            h = 2 * g + r
            scal, across = col[h], row[h]
            cum, query_unit = scal[:, 0:1], scal[:, 3:4]
            within = jnp.where(i >= j, jnp.exp(jnp.where(i >= j, cum - across[0:1], 0.0)), 0.0) * across[2:3]
            local = mm((within * query_key * query_unit).astype(BF16), solutions[h])
            own[h] = local[:, :WIDTH]
            reach[h] = (query.astype(F32) * (jnp.exp(cum) * query_unit) - local[:, WIDTH:]).astype(BF16)
            gated = ext[8 : 8 + length, gate_place(h)]
            ext[8 : 8 + length, gate_place(h)] = gain_ref[...] * (gated * sigmoid(gated))
        return carry

    def finish(h):
        core = (own[h] + mm(reach[h], s_in[h])).astype(BF16).astype(F32)
        gated = ext[8 : 8 + length, gate_place(h)]
        scaled = core * lax.rsqrt(jnp.mean(core * core, axis=1, keepdims=True) + EPSILON)
        normed[:, pl.ds(pl.multiple_of(h * WIDTH, WIDTH), WIDTH)] = (
            scaled * gated
        ).astype(BF16)

    early = ctx < n_ctx // 2 - 1

    @pl.when(jnp.logical_not(early))
    def _():
        lax.fori_loop(0, key_heads, within_block, 0)

    for h in range(heads):
        @pl.when(ctx > 0)
        def _():
            state_copy(h).wait_recv()

        @pl.when(ctx == 0)
        def _():
            s_in[h] = jnp.zeros((WIDTH, WIDTH), BF16)

        @pl.when(ctx < n_ctx - 1)
        def _():
            before = s_in[h]
            after = decay_all[h, 0:1, :] * before.astype(F32) - mm(minus[h], before) + inject[h]
            s_out[h] = after.astype(BF16)
            state_copy(h).start()

        @pl.when(ctx == n_ctx - 1)
        def _():
            finish(h)

    @pl.when(early)
    def _():
        lax.fori_loop(0, key_heads, within_block, 0)

    @pl.when(ctx < n_ctx - 1)
    def _():
        def one(h, carry):
            finish(h)
            return carry

        lax.fori_loop(0, heads, one, 0)

    wo_copy.wait()
    pieces = rs_send.shape[0]
    piece = depth // pieces

    def share_copy(q, k):
        peer = lax.rem(tp + k + 1, n_tp)
        place = pl.ds(q * piece, piece)
        return pltpu.make_async_remote_copy(
            src_ref=stage.at[pl.ds(pl.multiple_of(peer * rows, 16), rows), place],
            dst_ref=landed.at[k, :, place],
            send_sem=rs_send.at[q, k], recv_sem=rs_recv.at[q, k],
            device_id={"tp": peer}, device_id_type=MESH,
        )

    for q in range(pieces):
        for t in range(0, piece, 256):
            place = slice(q * piece + t, q * piece + t + 256)
            stage[:, place] = mm(normed[...], wo[:, place]).astype(BF16)
        for k in range(n_tp - 1):
            share_copy(q, k).start()
    for q in range(pieces):
        place = slice(q * piece, (q + 1) * piece)
        total = stage[mine, place].astype(F32)
        for k in range(n_tp - 1):
            share_copy(q, k).wait_recv()
            total = total + landed[k, :, place].astype(F32)
        out_ref[:, place] = total.astype(BF16)
    for q in range(pieces):
        for k in range(n_tp - 1):
            share_copy(q, k).wait_send()
    for copy in sent:
        copy.wait_send()

    @pl.when(ctx < n_ctx - 1)
    def _():
        border_copy.wait_send()
        for h in range(heads):
            state_copy(h).wait_send()


def on_device(tokens, w_project, w_mixers, conv_weight, decay_log, step_bias, norm_gain, w_output):
    n_ctx, n_tp = lax.axis_size("ctx"), lax.axis_size("tp")
    rows, depth = tokens.shape
    length = rows * n_tp
    key_heads = conv_weight.shape[0]
    heads = 2 * key_heads
    inner = heads * WIDTH
    batch = next(n for n in (4, 2, 1) if key_heads % n == 0)
    pieces = 4
    chunks = 4
    ways = 3 if n_tp == 4 else n_tp - 1
    vmem = pl.BlockSpec(memory_space=pltpu.VMEM)
    far = pl.BlockSpec(memory_space=pl.ANY)
    dma = pltpu.SemaphoreType.DMA
    square = (heads, WIDTH, WIDTH)
    return pl.pallas_call(
        functools.partial(kernel, n_ctx, n_tp, key_heads, batch, chunks),
        out_shape=jax.ShapeDtypeStruct((rows, depth), BF16),
        in_specs=[far] * 8,
        out_specs=vmem,
        scratch_shapes=[
            pltpu.VMEM((length, depth), BF16),
            pltpu.VMEM(w_project.shape, BF16),
            pltpu.VMEM((w_mixers.shape[1], depth), BF16),
            pltpu.VMEM(w_output.shape, BF16),
            pltpu.VMEM(conv_weight.shape, BF16),
            pltpu.SMEM((heads,), F32),
            pltpu.SMEM((heads,), F32),
            pltpu.VMEM((1, WIDTH), F32),
            pltpu.VMEM((8 + length, key_heads * 6 * WIDTH), F32),
            pltpu.VMEM((length, key_heads * 4 * WIDTH), BF16),
            pltpu.VMEM((BORDER, key_heads * 4 * WIDTH), BF16),
            pltpu.VMEM((BORDER, key_heads * 4 * WIDTH), BF16),
            pltpu.VMEM((heads, length, WIDTH), F32),
            pltpu.VMEM((heads, 8, length), F32),
            pltpu.VMEM((heads, length, 2 * WIDTH), BF16),
            pltpu.VMEM(square, BF16),
            pltpu.VMEM(square, F32),
            pltpu.VMEM((heads, length, WIDTH), F32),
            pltpu.VMEM((heads, length, WIDTH), BF16),
            pltpu.VMEM(square, BF16),
            pltpu.VMEM(square, BF16),
            pltpu.VMEM((heads, 8, WIDTH), F32),
            pltpu.VMEM((length, inner), BF16),
            pltpu.VMEM((length, depth), BF16),
            pltpu.VMEM((n_tp - 1, rows, depth), BF16),
            dma, dma((chunks,)), dma((5,)), dma,
            dma((ways, chunks)), dma((ways, chunks)), dma((2,)),
            dma((heads,)), dma((heads,)),
            dma((pieces, n_tp - 1)), dma((pieces, n_tp - 1)),
        ],
        compiler_params=pltpu.CompilerParams(
            collective_id=0, has_side_effects=True, vmem_limit_bytes=63 * 1024 * 1024
        ),
    )(
        tokens, w_project, w_mixers.T, conv_weight, decay_log, step_bias, norm_gain.reshape(1, WIDTH), w_output,
    )


def solution(mesh):
    placed = (
        P(("ctx", "tp"), None),
        P(None, "tp"),
        P(None, "tp"),
        P("tp", None, None),
        P("tp"),
        P("tp"),
        P(),
        P("tp", None),
    )
    return jax.shard_map(
        on_device, mesh=mesh, in_specs=placed, out_specs=P(("ctx", "tp"), None), check_vma=False
    )
```

```python
import functools

import jax
import jax.numpy as jnp
from jax import lax
from jax.experimental import pallas as pl
from jax.experimental.pallas import tpu as pltpu
from jax.sharding import PartitionSpec as P

EPSILON = 1e-06
TOP_PRECISION = lax.Precision.HIGHEST
MESH = pl.DeviceIdType.MESH
WIDTH = 128
F32 = jnp.float32
BF16 = jnp.bfloat16
BORDER = 16
LEAST_LOG = -120.0


def mm(a, b):
    return jnp.dot(a, b, preferred_element_type=F32)


def mm_rows(a, b):
    return lax.dot_general(a, b, (((1,), (1,)), ((), ())), preferred_element_type=F32)


def mm_over_rows(a, b):
    return lax.dot_general(a, b, (((0,), (0,)), ((), ())), preferred_element_type=F32)


def sigmoid(x):
    return 1.0 / (1.0 + jnp.exp(-x))


def softplus(x):
    small = jnp.exp(-jnp.abs(x))
    grown = 1.0 + small
    tail = jnp.where(grown == 1.0, small, jnp.log(grown) * small / jnp.where(grown == 1.0, 1.0, grown - 1.0))
    return jnp.maximum(x, 0.0) + tail


def kernel(
    n_ctx, n_tp, key_heads, batch, chunks,
    tok_ref, wp_ref, wm_ref, cw_in, dl_in, sb_in, gain_in, wo_ref,
    out_ref,
    gath, wp, wm, wo, cw_ref, dl_ref, sb_ref, gain_ref,
    ext, act, border_out, border_in, col, row, solutions, minus, inject, own, reach,
    s_in, s_out, decay_all, normed, stage, landed,
    own_sem, wp_sem, small_sem, wo_sem, ag_send, ag_recv, border_sem, state_send, state_recv, rs_send, rs_recv,
):
    rows = tok_ref.shape[0]
    length = rows * n_tp
    heads = 2 * key_heads
    depth = wo_ref.shape[1]
    ctx, tp = lax.axis_index("ctx"), lax.axis_index("tp")
    six, four = 6 * WIDTH, 4 * WIDTH

    k_rows = depth // chunks
    small_copies = [
        pltpu.make_async_copy(source, target, small_sem.at[n])
        for n, (source, target) in enumerate(
            [(wm_ref, wm), (cw_in, cw_ref), (dl_in, dl_ref), (sb_in, sb_ref), (gain_in, gain_ref)]
        )
    ]
    wo_copy = pltpu.make_async_copy(wo_ref, wo, wo_sem)
    wp_copies = [
        pltpu.make_async_copy(wp_ref.at[pl.ds(k * k_rows, k_rows)], wp.at[pl.ds(k * k_rows, k_rows)], wp_sem.at[k])
        for k in range(chunks)
    ]
    mine = pl.ds(pl.multiple_of(tp * rows, 16), rows)
    own_copy = pltpu.make_async_copy(tok_ref, gath.at[mine], own_sem)
    own_copy.start()
    for copy in wp_copies[: chunks // 2]:
        copy.start()

    barrier = pltpu.get_barrier_semaphore()
    peers = [lax.rem(tp + k, n_tp) for k in range(1, n_tp)]
    for peer in peers:
        pl.semaphore_signal(barrier, inc=1, device_id={"tp": peer}, device_id_type=MESH)

    @pl.when(ctx > 0)
    def _():
        pl.semaphore_signal(barrier, inc=1, device_id={"ctx": ctx - 1}, device_id_type=MESH)

    @pl.when(ctx < n_ctx - 1)
    def _():
        pl.semaphore_signal(barrier, inc=1, device_id={"ctx": ctx + 1}, device_id_type=MESH)

    beside = jnp.where(ctx > 0, 1, 0) + jnp.where(ctx < n_ctx - 1, 1, 0)
    pl.semaphore_wait(barrier, n_tp - 1 + beside)

    def block_copy(source, held, peer, way, k):
        place = pl.ds(k * k_rows, k_rows)
        return pltpu.make_async_remote_copy(
            src_ref=source.at[:, place] if held is mine else source.at[held, place],
            dst_ref=gath.at[held, place],
            send_sem=ag_send.at[way, k], recv_sem=ag_recv.at[way, k],
            device_id={"tp": peer}, device_id_type=MESH,
        )

    def project(half):
        groups = chunks // 2
        for k in range(half * groups, (half + 1) * groups):
            wp_copies[k].wait()
        place = slice(half * groups * k_rows, (half + 1) * groups * k_rows)
        total_columns = key_heads * six
        for start in range(0, total_columns, 256):
            span = slice(start, start + 256)
            part = mm(gath[:, place], wp[place, span])
            if half == 1:
                part = (part + ext[8 : 8 + length, span]).astype(BF16).astype(F32)
            ext[8 : 8 + length, span] = part

    def start_rest():
        for copy in wp_copies[chunks // 2 :]:
            copy.start()
        for copy in small_copies:
            copy.start()
        wo_copy.start()

    if n_tp == 4:
        x_peer = tp + 1 - 2 * lax.rem(tp, 2)
        y_peer = lax.rem(tp + 2, 4)
        x_rows = pl.ds(pl.multiple_of(x_peer * rows, 16), rows)
        y_rows = pl.ds(pl.multiple_of(y_peer * rows, 16), rows)
        direct = [
            [block_copy(tok_ref, mine, peer, way, k) for way, peer in enumerate((x_peer, y_peer))]
            for k in range(chunks)
        ]
        passed = [
            block_copy(gath, x_rows, y_peer, 2, k) if k % 2 == 0 else block_copy(gath, y_rows, x_peer, 2, k)
            for k in range(chunks)
        ]
        for pair in direct:
            for copy in pair:
                copy.start()
        start_rest()
        own_copy.wait()
        for k in range(chunks):
            for copy in direct[k]:
                copy.wait_recv()
            passed[k].start()
            if k == chunks - 1:
                for early_copy in passed[: chunks // 2]:
                    early_copy.wait_recv()
                project(0)
        for late_copy in passed[chunks // 2 :]:
            late_copy.wait_recv()
        project(1)
        sent = [copy for pair in direct for copy in pair] + passed
    else:
        sent = [block_copy(tok_ref, mine, peer, way, k) for k in range(chunks) for way, peer in enumerate(peers)]
        for copy in sent:
            copy.start()
        start_rest()
        own_copy.wait()
        for k in range(chunks):
            for way in range(n_tp - 1):
                sent[k * (n_tp - 1) + way].wait_recv()
            if (k + 1) % (chunks // 2) == 0:
                project((k + 1) // (chunks // 2) - 1)

    for g in range(key_heads):
        border_out[:, g * four : (g + 1) * four] = ext[
            8 + length - BORDER : 8 + length, g * six : g * six + four
        ].astype(BF16)
    border_copy = pltpu.make_async_remote_copy(
        src_ref=border_out, dst_ref=border_in, send_sem=border_sem.at[0], recv_sem=border_sem.at[1],
        device_id={"ctx": lax.rem(ctx + 1, n_ctx)}, device_id_type=MESH,
    )

    @pl.when(ctx < n_ctx - 1)
    def _():
        border_copy.start()

    for copy in small_copies:
        copy.wait()
    mixers = mm_rows(gath[...], wm[...]).astype(BF16).astype(F32)
    columns = mixers.shape[1]
    lane = lax.broadcasted_iota(jnp.int32, (1, columns), 1)
    rate = jnp.zeros((1, columns), F32)
    bias = jnp.zeros((1, columns), F32)
    for h in range(heads):
        here = lane == 4 * (h // 2) + 2 + h % 2
        rate = jnp.where(here, dl_ref[h], rate)
        bias = jnp.where(here, sb_ref[h], bias)
    strength = sigmoid(mixers)
    log_decay = jnp.maximum(-jnp.exp(rate) * softplus(mixers + bias), LEAST_LOG)
    at_row = lax.broadcasted_iota(jnp.int32, (length, length), 0)
    at_col = lax.broadcasted_iota(jnp.int32, (length, length), 1)
    lower = jnp.where(at_row >= at_col, 1.0, 0.0)
    cumulative = jnp.dot(lower, log_decay, precision=TOP_PRECISION, preferred_element_type=F32)

    ext[0:8, :] = jnp.zeros((8, ext.shape[1]), F32)

    def convolve(count):
        def one(g, carry):
            for t in range(4):
                place = pl.ds(pl.multiple_of(g * six + t * WIDTH, WIDTH), WIDTH)
                taps = cw_ref[g, :, t * WIDTH : (t + 1) * WIDTH].astype(F32)
                total = taps[0:1] * ext[5 : 5 + count, place]
                for j in range(1, 4):
                    total = total + taps[j : j + 1] * ext[5 + j : 5 + j + count, place]
                target = pl.ds(pl.multiple_of(g * four + t * WIDTH, WIDTH), WIDTH)
                act[0:count, target] = (total * sigmoid(total)).astype(BF16)
            return carry

        lax.fori_loop(0, key_heads, one, 0)

    convolve(length)

    @pl.when(ctx > 0)
    def _():
        border_copy.wait_recv()
        for g in range(key_heads):
            ext[0:8, g * six : g * six + four] = border_in[BORDER - 8 : BORDER, g * four : (g + 1) * four].astype(F32)
        convolve(BORDER)

    wide = lax.broadcasted_iota(jnp.int32, (length, WIDTH), 1)
    for g in range(key_heads):
        query = act[:, g * four : g * four + WIDTH].astype(F32)
        key = act[:, g * four + WIDTH : g * four + 2 * WIDTH].astype(F32)
        query_unit = lax.rsqrt(jnp.sum(query * query, axis=1, keepdims=True) + EPSILON)
        key_unit = lax.rsqrt(jnp.sum(key * key, axis=1, keepdims=True) + EPSILON)
        for r in range(2):
            h = 2 * g + r
            cum = cumulative[:, 4 * g + 2 + r : 4 * g + 3 + r]
            beta = strength[:, 4 * g + r : 4 * g + r + 1]
            packed = jnp.where(
                wide == 0, cum, jnp.where(wide == 1, beta, jnp.where(wide == 2, key_unit, query_unit))
            )
            col[h] = packed
            row[h] = jnp.transpose(packed)[0:8]

    def heads_of(step, carry):
        i = lax.broadcasted_iota(jnp.int32, (length, length), 0)
        j = lax.broadcasted_iota(jnp.int32, (length, length), 1)
        apart = jnp.bitwise_xor(i, j)
        lows, inverses = [], []
        for b in range(batch):
            g = step * batch + b
            key = act[:, pl.ds(pl.multiple_of(g * four + WIDTH, WIDTH), WIDTH)]
            key_key = mm_rows(key, key)
            for r in range(2):
                h = 2 * g + r
                scal, across = col[h], row[h]
                cum, beta, key_unit = (scal[:, n : n + 1] for n in range(3))
                within = jnp.exp(jnp.where(i > j, cum - across[0:1], 0.0)) * across[2:3]
                low = jnp.where(i > j, within * key_key * (beta * key_unit), 0.0).astype(BF16)
                lows.append(low)
                inverses.append(jnp.where(i == j, 1.0, jnp.where(apart == 1, -low.astype(F32), 0.0)).astype(BF16))
        span = 2
        while span < length:
            between = jnp.where((apart >= span) & (apart < 2 * span), 1.0, 0.0).astype(BF16)
            firsts = [mm(t, low * between).astype(BF16) for t, low in zip(inverses, lows)]
            inverses = [t - mm(first, t).astype(BF16) for t, first in zip(inverses, firsts)]
            span *= 2
        for n, inverse in enumerate(inverses):
            g = step * batch + n // 2
            r = n % 2
            h = 2 * g + r
            scal = col[h]
            cum, beta, key_unit = (scal[:, m : m + 1] for m in range(3))
            key = act[:, pl.ds(pl.multiple_of(g * four + WIDTH, WIDTH), WIDTH)].astype(F32)
            vector = act[:, pl.ds(pl.multiple_of(g * four + (2 + r) * WIDTH, WIDTH), WIDTH)].astype(F32)
            last = cum[length - 1 : length]
            right = jnp.concatenate([vector * beta, key * (beta * jnp.exp(cum) * key_unit)], axis=1).astype(BF16)
            solved = mm(inverse, right).astype(BF16)
            solutions[h] = solved
            tail = (key * (jnp.exp(last - cum) * key_unit)).astype(BF16)
            ends = mm_over_rows(tail, solved)
            inject[h] = ends[:, :WIDTH]
            minus[h] = ends[:, WIDTH:].astype(BF16)
            decay_all[h] = jnp.broadcast_to(jnp.exp(last), (8, WIDTH))
        return carry

    lax.fori_loop(0, key_heads // batch, heads_of, 0)

    def state_copy(h):
        return pltpu.make_async_remote_copy(
            src_ref=s_out.at[h], dst_ref=s_in.at[h], send_sem=state_send.at[h], recv_sem=state_recv.at[h],
            device_id={"ctx": lax.rem(ctx + 1, n_ctx)}, device_id_type=MESH,
        )

    def gate_place(h):
        return pl.ds(pl.multiple_of((h // 2) * six + four + (h % 2) * WIDTH, WIDTH), WIDTH)

    def within_block(g, carry):
        i = lax.broadcasted_iota(jnp.int32, (length, length), 0)
        j = lax.broadcasted_iota(jnp.int32, (length, length), 1)
        query = act[:, pl.ds(pl.multiple_of(g * four, WIDTH), WIDTH)]
        key = act[:, pl.ds(pl.multiple_of(g * four + WIDTH, WIDTH), WIDTH)]
        query_key = mm_rows(query, key)
        for r in range(2):
            h = 2 * g + r
            scal, across = col[h], row[h]
            cum, query_unit = scal[:, 0:1], scal[:, 3:4]
            within = jnp.where(i >= j, jnp.exp(jnp.where(i >= j, cum - across[0:1], 0.0)), 0.0) * across[2:3]
            local = mm((within * query_key * query_unit).astype(BF16), solutions[h])
            own[h] = local[:, :WIDTH]
            reach[h] = (query.astype(F32) * (jnp.exp(cum) * query_unit) - local[:, WIDTH:]).astype(BF16)
            gated = ext[8 : 8 + length, gate_place(h)]
            ext[8 : 8 + length, gate_place(h)] = gain_ref[...] * (gated * sigmoid(gated))
        return carry

    def finish(h):
        core = (own[h] + mm(reach[h], s_in[h])).astype(BF16).astype(F32)
        gated = ext[8 : 8 + length, gate_place(h)]
        scaled = core * lax.rsqrt(jnp.mean(core * core, axis=1, keepdims=True) + EPSILON)
        normed[:, pl.ds(pl.multiple_of(h * WIDTH, WIDTH), WIDTH)] = (
            scaled * gated
        ).astype(BF16)

    early = ctx < n_ctx // 2 - 1

    @pl.when(jnp.logical_not(early))
    def _():
        lax.fori_loop(0, key_heads, within_block, 0)

    for h in range(heads):
        @pl.when(ctx > 0)
        def _():
            state_copy(h).wait_recv()

        @pl.when(ctx == 0)
        def _():
            s_in[h] = jnp.zeros((WIDTH, WIDTH), BF16)

        @pl.when(ctx < n_ctx - 1)
        def _():
            before = s_in[h]
            after = decay_all[h, 0:1, :] * before.astype(F32) - mm(minus[h], before) + inject[h]
            s_out[h] = after.astype(BF16)
            state_copy(h).start()

        @pl.when(ctx == n_ctx - 1)
        def _():
            finish(h)

    @pl.when(early)
    def _():
        lax.fori_loop(0, key_heads, within_block, 0)

    @pl.when(ctx < n_ctx - 1)
    def _():
        for h in range(heads):
            finish(h)

    wo_copy.wait()
    pieces = rs_send.shape[0]
    piece = depth // pieces

    def share_copy(q, k):
        peer = lax.rem(tp + k + 1, n_tp)
        place = pl.ds(q * piece, piece)
        return pltpu.make_async_remote_copy(
            src_ref=stage.at[pl.ds(pl.multiple_of(peer * rows, 16), rows), place],
            dst_ref=landed.at[k, :, place],
            send_sem=rs_send.at[q, k], recv_sem=rs_recv.at[q, k],
            device_id={"tp": peer}, device_id_type=MESH,
        )

    for q in range(pieces):
        for t in range(0, piece, 256):
            place = slice(q * piece + t, q * piece + t + 256)
            stage[:, place] = mm(normed[...], wo[:, place]).astype(BF16)
        for k in range(n_tp - 1):
            share_copy(q, k).start()
    for q in range(pieces):
        place = slice(q * piece, (q + 1) * piece)
        total = stage[mine, place].astype(F32)
        for k in range(n_tp - 1):
            share_copy(q, k).wait_recv()
            total = total + landed[k, :, place].astype(F32)
        out_ref[:, place] = total.astype(BF16)
    for q in range(pieces):
        for k in range(n_tp - 1):
            share_copy(q, k).wait_send()
    for copy in sent:
        copy.wait_send()

    @pl.when(ctx < n_ctx - 1)
    def _():
        border_copy.wait_send()
        for h in range(heads):
            state_copy(h).wait_send()


def on_device(tokens, w_project, w_mixers, conv_weight, decay_log, step_bias, norm_gain, w_output):
    n_ctx, n_tp = lax.axis_size("ctx"), lax.axis_size("tp")
    rows, depth = tokens.shape
    length = rows * n_tp
    key_heads = conv_weight.shape[0]
    heads = 2 * key_heads
    inner = heads * WIDTH
    batch = next(n for n in (4, 2, 1) if key_heads % n == 0)
    pieces = 4
    chunks = 4
    ways = 3 if n_tp == 4 else n_tp - 1
    vmem = pl.BlockSpec(memory_space=pltpu.VMEM)
    far = pl.BlockSpec(memory_space=pl.ANY)
    dma = pltpu.SemaphoreType.DMA
    square = (heads, WIDTH, WIDTH)
    return pl.pallas_call(
        functools.partial(kernel, n_ctx, n_tp, key_heads, batch, chunks),
        out_shape=jax.ShapeDtypeStruct((rows, depth), BF16),
        in_specs=[far] * 8,
        out_specs=vmem,
        scratch_shapes=[
            pltpu.VMEM((length, depth), BF16),
            pltpu.VMEM(w_project.shape, BF16),
            pltpu.VMEM((w_mixers.shape[1], depth), BF16),
            pltpu.VMEM(w_output.shape, BF16),
            pltpu.VMEM(conv_weight.shape, BF16),
            pltpu.SMEM((heads,), F32),
            pltpu.SMEM((heads,), F32),
            pltpu.VMEM((1, WIDTH), F32),
            pltpu.VMEM((8 + length, key_heads * 6 * WIDTH), F32),
            pltpu.VMEM((length, key_heads * 4 * WIDTH), BF16),
            pltpu.VMEM((BORDER, key_heads * 4 * WIDTH), BF16),
            pltpu.VMEM((BORDER, key_heads * 4 * WIDTH), BF16),
            pltpu.VMEM((heads, length, WIDTH), F32),
            pltpu.VMEM((heads, 8, length), F32),
            pltpu.VMEM((heads, length, 2 * WIDTH), BF16),
            pltpu.VMEM(square, BF16),
            pltpu.VMEM(square, F32),
            pltpu.VMEM((heads, length, WIDTH), F32),
            pltpu.VMEM((heads, length, WIDTH), BF16),
            pltpu.VMEM(square, BF16),
            pltpu.VMEM(square, BF16),
            pltpu.VMEM((heads, 8, WIDTH), F32),
            pltpu.VMEM((length, inner), BF16),
            pltpu.VMEM((length, depth), BF16),
            pltpu.VMEM((n_tp - 1, rows, depth), BF16),
            dma, dma((chunks,)), dma((5,)), dma,
            dma((ways, chunks)), dma((ways, chunks)), dma((2,)),
            dma((heads,)), dma((heads,)),
            dma((pieces, n_tp - 1)), dma((pieces, n_tp - 1)),
        ],
        compiler_params=pltpu.CompilerParams(
            collective_id=0, has_side_effects=True, vmem_limit_bytes=63 * 1024 * 1024
        ),
    )(
        tokens, w_project, w_mixers.T, conv_weight, decay_log, step_bias, norm_gain.reshape(1, WIDTH), w_output,
    )


def solution(mesh):
    placed = (
        P(("ctx", "tp"), None),
        P(None, "tp"),
        P(None, "tp"),
        P("tp", None, None),
        P("tp"),
        P("tp"),
        P(),
        P("tp", None),
    )
    return jax.shard_map(
        on_device, mesh=mesh, in_specs=placed, out_specs=P(("ctx", "tp"), None), check_vma=False
    )
```
